32 devices in a mesh: dp: 2 (over core), head: 4 (over y, x), ctx: 4 (over z).
Axes of the slice: x: 2, y: 2, z: 4, core: 2. Of those that a mesh axis runs over, the one named last changes fastest.
Arguments:
- q_raw: bfloat16 [2, 512, 4096], P('dp', 'ctx', 'head'), may hold values from -6 to 6
- k_raw: bfloat16 [2, 512, 4096], P('dp', 'ctx', 'head'), may hold values from -6 to 6
- v_raw: bfloat16 [2, 512, 4096], P('dp', 'ctx', 'head'), may hold values from -6 to 6
- conv_weight: float32 [3, 4, 4096], P(None, None, 'head'), may hold values from -4 to 4
- decay_logit: float32 [2, 512, 32], P('dp', 'ctx', 'head'), may hold values from -8 to 8
- beta_logit: float32 [2, 512, 32], P('dp', 'ctx', 'head'), may hold values from -8 to 8
- decay_rate: float32 [32], P('head'), may hold values from 0.00048828125 to 0.05
- block_resets: int32 [2, 4], P('dp', 'ctx'), may hold values from 0 to 1
- norm_gain: float32 [4096], P('head'), may hold values from 0.25 to 1.75
- d_out: bfloat16 [2, 512, 4096], P('dp', 'ctx', 'head'), may hold values from -6 to 6
Outputs:
- out: bfloat16 [2, 512, 4096], P('dp', 'ctx', 'head')
- d_q_raw: bfloat16 [2, 512, 4096], P('dp', 'ctx', 'head')
- d_k_raw: bfloat16 [2, 512, 4096], P('dp', 'ctx', 'head')
- d_v_raw: bfloat16 [2, 512, 4096], P('dp', 'ctx', 'head')
- d_conv_weight: float32 [3, 4, 4096], P(None, None, 'head')
- d_decay_logit: float32 [2, 512, 32], P('dp', 'ctx', 'head')
- d_beta_logit: float32 [2, 512, 32], P('dp', 'ctx', 'head')
- d_decay_rate: float32 [32], P('head')
- d_norm_gain: float32 [4096], P('head')
The draws below stay inside these ranges and needn't reach their ends.
All inputs are finite; a program needn't handle non-finite values.
Results may differ from the reference program's by a relative error of at most 0.0019.
Values may be sent and summed in bfloat16 or wider, within the bound.
A program may use at most 128 MiB of HBM per device.

```python
import jax
import jax.numpy as jnp
from jax import lax

DK = 128
HEAD_COUNT = 32
TAPS = 4
BLOCK_LENGTH = 128
TOK_DEV = 128
SEQUENCE_LENGTH = 512
BATCH_COUNT = 2


def slow_heads(key):
    picks = jax.random.randint(jax.random.fold_in(key, 11), (HEAD_COUNT,), 0, 8)
    return picks < 4


def draw_decay_rate(key, part):
    sluggish_decay = slow_heads(key)
    spread = jax.random.uniform(jax.random.fold_in(key, 12), (HEAD_COUNT,), jnp.float32)
    slow_rate = 0.25 / SEQUENCE_LENGTH * jnp.exp(spread * jnp.log(4.0))
    fast_rate = 0.02 * jnp.exp(spread * jnp.log(2.5))
    return jnp.where(sluggish_decay, slow_rate, fast_rate).astype(jnp.float32)


def draw_decay_logit(key, part):
    shape = (BATCH_COUNT, SEQUENCE_LENGTH, HEAD_COUNT)
    base = jnp.clip(1.5 * jax.random.normal(jax.random.fold_in(key, 21), shape, jnp.float32), -8.0, 8.0)
    ranges = SEQUENCE_LENGTH // TOK_DEV
    span = min(6, ranges)
    first = jax.random.randint(jax.random.fold_in(key, 22), (BATCH_COUNT, 1, HEAD_COUNT), 0, ranges)
    which = (jnp.arange(SEQUENCE_LENGTH) // TOK_DEV)[None, :, None]
    inside = (which >= first) & (which < first + span)
    holding = jax.random.uniform(jax.random.fold_in(key, 23), shape, jnp.float32, -8.0, -7.0)
    return jnp.where(inside, holding, base).astype(jnp.float32)


def draw_beta_logit(key, part):
    sluggish_decay = slow_heads(key)
    shape = (BATCH_COUNT, SEQUENCE_LENGTH, HEAD_COUNT)
    weak = jax.random.uniform(jax.random.fold_in(key, 13), shape, jnp.float32, -6.0, -4.0)
    strong = jnp.clip(1.5 * jax.random.normal(jax.random.fold_in(key, 14), shape, jnp.float32), -8.0, 8.0)
    sudden_spike = jax.random.randint(jax.random.fold_in(key, 17), (BATCH_COUNT, SEQUENCE_LENGTH // BLOCK_LENGTH, HEAD_COUNT), 0, 8) == 0
    spike_rows = jnp.repeat(sudden_spike, BLOCK_LENGTH, axis=1)
    retain_faint = sluggish_decay[None, None, :] & jnp.logical_not(spike_rows)
    return jnp.where(retain_faint, weak, strong).astype(jnp.float32)


def draw_block_resets(key, part):
    count = SEQUENCE_LENGTH // BLOCK_LENGTH
    flags = (jax.random.randint(jax.random.fold_in(key, 15), (BATCH_COUNT, count), 0, 256) == 0).astype(jnp.int32)
    planted = jax.random.randint(jax.random.fold_in(key, 16), (), 1, count)
    marked = (jnp.arange(count)[None, :] == planted) & (jnp.arange(BATCH_COUNT)[:, None] == 0)
    return jnp.maximum(flags, marked.astype(jnp.int32))


def block_scale(own_key, extent, cuts, low, top_value):
    level = 1.0
    for dim, parts in cuts:
        draws = jax.random.uniform(jax.random.fold_in(jax.random.fold_in(own_key, 6), dim), (parts,), jnp.float32, low / len(cuts), top_value / len(cuts))
        level = level * jnp.repeat(jnp.exp(draws), extent[dim] // parts).reshape((-1,) + (1,) * (len(extent) - 1 - dim))
    return level


def gaussian(rng, shape, deviation, reach, shards=(), held_as=jnp.bfloat16):
    drawn = deviation * jax.random.normal(rng, shape, jnp.float32)
    if shards:
        drawn = drawn * block_scale(rng, shape, shards, -0.22, 0.18)
    return jnp.clip(drawn, -reach, reach).astype(held_as)


def setup_inputs(seed: int = 0) -> dict:
    keys = jax.random.split(jax.random.key(seed), 11)
    q_raw = gaussian(keys[0], (BATCH_COUNT, SEQUENCE_LENGTH, HEAD_COUNT * DK), 1.0, 6.0, ((0, 2), (1, 4), (2, 4)))
    k_raw = gaussian(keys[1], (BATCH_COUNT, SEQUENCE_LENGTH, HEAD_COUNT * DK), 1.0, 6.0, ((0, 2), (1, 4), (2, 4)))
    v_raw = gaussian(keys[2], (BATCH_COUNT, SEQUENCE_LENGTH, HEAD_COUNT * DK), 1.0, 6.0, ((0, 2), (1, 4), (2, 4)))
    conv_weight = gaussian(keys[3], (3, TAPS, HEAD_COUNT * DK), 2 ** -0.5, 4.0, ((2, 4),), jnp.float32)
    decay_logit = draw_decay_logit(jax.random.fold_in(keys[10], 71), 0)
    beta_logit = draw_beta_logit(jax.random.fold_in(keys[10], 71), 0)
    decay_rate = draw_decay_rate(jax.random.fold_in(keys[10], 71), 0)
    block_resets = draw_block_resets(jax.random.fold_in(keys[10], 71), 0)
    norm_gain = jnp.clip(1.0 + 0.15 * jax.random.normal(keys[8], (HEAD_COUNT * DK,), jnp.float32), 0.25, 1.75)
    d_out = gaussian(keys[9], (BATCH_COUNT, SEQUENCE_LENGTH, HEAD_COUNT * DK), 1.0, 6.0, ((0, 2), (1, 4), (2, 4)))
    return {"q_raw": q_raw, "k_raw": k_raw, "v_raw": v_raw, "conv_weight": conv_weight, "decay_logit": decay_logit, "beta_logit": beta_logit, "decay_rate": decay_rate, "block_resets": block_resets, "norm_gain": norm_gain, "d_out": d_out}


highest = lax.Precision.HIGHEST

def conv_act(padded, weight, resets, block):
    taps = weight.shape[1]
    length = padded.shape[1] - taps + 1
    position = jnp.arange(length) % block
    flags = jnp.repeat(resets.astype(jnp.float32), block)
    total = jnp.zeros((padded.shape[0], length, padded.shape[2]), jnp.float32)
    for tap_index in range(taps):
        valid = 1.0 - flags * (position < tap_index).astype(jnp.float32)
        offset = taps - 1 - tap_index
        total = total + weight[:, tap_index][:, None, :] * padded[:, offset:offset + length] * valid[None, :, None]
    return jax.nn.silu(total)

def features(activated, logits_decay, logits_write, rates, heads):
    length = activated.shape[1]
    size_key = activated.shape[2] // heads

    def unit(array):
        return array * lax.rsqrt(lax.optimization_barrier(jnp.sum(array * array, axis=-1, keepdims=True)) + 1e-06)
    queries = unit(activated[0].reshape(length, heads, size_key)) * size_key ** (-0.5)
    key_rows = unit(activated[1].reshape(length, heads, size_key))
    values = activated[2].reshape(length, heads, size_key)
    gate_log = -rates[None, :] * jax.nn.softplus(logits_decay)
    strength = jax.nn.sigmoid(logits_write)
    return (queries, key_rows, values, gate_log, strength)

def block_run(queries, key_rows, values, gate_log, strength, resets, initial, block):
    length, heads, size_key = queries.shape
    width_value = values.shape[-1]
    count = length // block

    def split(array):
        return array.reshape((count, block) + array.shape[1:])
    index = jnp.arange(block)
    strict = index[:, None] > index[None, :]
    inclusive = index[:, None] >= index[None, :]
    identity = jnp.eye(block, dtype=jnp.float32)

    def advance(state, inputs):
        query_blk, key_blk, value_blk, gate_blk, write_blk, reset_blk = inputs
        state = state * (1 - reset_blk).astype(jnp.float32)
        cumul = jnp.cumsum(gate_blk, axis=0).T
        spread = cumul[:, :, None] - cumul[:, None, :]
        lower_decay = jnp.where(strict, jnp.exp(jnp.where(strict, spread, 0.0)), 0.0)
        upper_decay = jnp.where(inclusive, jnp.exp(jnp.where(inclusive, spread, 0.0)), 0.0)
        writes = write_blk.T
        key_key = jnp.einsum('thd,shd->hts', key_blk, key_blk, precision=highest)
        system = lower_decay * key_key * writes[:, None, :] + identity
        growth = jnp.exp(cumul)
        key_state = jnp.einsum('thd,hvd->htv', key_blk, state, precision=highest)
        right_side = jnp.transpose(value_blk, (1, 0, 2)) - growth[:, :, None] * key_state
        deltas = lax.linalg.triangular_solve(system, right_side, left_side=True, lower=True, unit_diagonal=True)
        weighted = deltas * writes[:, :, None]
        query_key = jnp.einsum('thd,shd->hts', query_blk, key_blk, precision=highest)
        query_state = jnp.einsum('thd,hvd->htv', query_blk, state, precision=highest)
        mixed = growth[:, :, None] * query_state + jnp.einsum('hts,hsv->htv', upper_decay * query_key, weighted, precision=highest)
        tail_decay = jnp.exp(cumul[:, -1:] - cumul)
        state = jnp.exp(cumul[:, -1])[:, None, None] * state + jnp.einsum('hsv,shd->hvd', weighted * tail_decay[:, :, None], key_blk, precision=highest)
        return (state, jnp.transpose(mixed, (1, 0, 2)))
    final, outputs = lax.scan(jax.checkpoint(advance), initial, (split(queries), split(key_rows), split(values), split(gate_log), split(strength), resets))
    return (outputs.reshape(length, heads, width_value), final)

def sequence_out(q_row, k_row, v_row, weight, logits_decay, logits_write, rates, resets, gain):
    taps = weight.shape[1]
    stacked = jnp.stack([q_row, k_row, v_row])
    padded = jnp.pad(stacked, ((0, 0), (taps - 1, 0), (0, 0)))
    activated = conv_act(padded, weight, resets, BLOCK_LENGTH)
    queries, key_rows, values, gate_log, strength = features(activated, logits_decay, logits_write, rates, HEAD_COUNT)
    initial = jnp.zeros((HEAD_COUNT, DK, DK), jnp.float32)
    mixed, final = block_run(queries, key_rows, values, gate_log, strength, resets, initial, BLOCK_LENGTH)
    flat = mixed.reshape(SEQUENCE_LENGTH, HEAD_COUNT * DK)
    row_scale = lax.rsqrt(lax.optimization_barrier(jnp.mean(flat * flat, axis=1)) + 1e-06)
    return flat * row_scale[:, None] * gain[None, :]

def reference(q_raw, k_raw, v_raw, conv_weight, decay_logit, beta_logit, decay_rate, block_resets, norm_gain, d_out):

    def whole(q_all, k_all, v_all, weight, logits_decay, logits_write, rates, gain):
        mapped = jax.vmap(sequence_out, in_axes=(0, 0, 0, None, 0, 0, None, 0, None))
        return mapped(q_all, k_all, v_all, weight, logits_decay, logits_write, rates, block_resets, gain)
    result, pullback = jax.vjp(whole, q_raw.astype(jnp.float32), k_raw.astype(jnp.float32), v_raw.astype(jnp.float32), conv_weight, decay_logit, beta_logit, decay_rate, norm_gain)
    grads = pullback(d_out.astype(jnp.float32))
    return (result.astype(jnp.bfloat16), grads[0].astype(jnp.bfloat16), grads[1].astype(jnp.bfloat16), grads[2].astype(jnp.bfloat16), grads[3], grads[4], grads[5], grads[6], grads[7])
```

```python
import functools

import jax
import jax.numpy as jnp
from jax import lax
from jax.experimental import pallas as pl
from jax.experimental.pallas import tpu as pltpu
from jax.sharding import PartitionSpec as P

F32 = jnp.float32
BF16 = jnp.bfloat16
MESH = pl.DeviceIdType.MESH
VMEM_BYTES = 56 * 1024 * 1024
TILE = 16
EPS = 1e-06


def pair(x):
    hi = x.astype(BF16)
    return hi, (x - hi.astype(F32)).astype(BF16)


def dot_dims(a, b, dims):
    return lax.dot_general(a, b, (dims, ((), ())), preferred_element_type=F32)


def dot3(a, b, dims):
    return dot_dims(a[0], b[0], dims) + (dot_dims(a[0], b[1], dims) + dot_dims(a[1], b[0], dims))


NN = ((1,), (0,))
NT = ((1,), (1,))
TN = ((0,), (0,))


def iota(shape, dim):
    return lax.broadcasted_iota(jnp.int32, shape, dim)


def rows_sum(x):
    return jnp.sum(x, axis=1, keepdims=True)


def gates(logit, rate):
    soft = jnp.maximum(logit, 0.0) + jnp.log1p(jnp.exp(-jnp.abs(logit)))
    return soft, -rate * soft


def triple(x):
    hi, rest = pair(x)
    lo = (x - hi.astype(F32) - rest.astype(F32)).astype(BF16)
    return hi, rest, lo


def cumul_forms(gate):
    length = gate.shape[0]
    lower = (iota((length, length), 0) >= iota((length, length), 1)).astype(F32).astype(BF16)
    parts = triple(gate)
    col = sum(dot_dims(lower, p, NN) for p in parts)
    row = sum(dot_dims(p, lower, ((0,), (1,))) for p in parts)
    return col, row


def pick_col(x, lane):
    return rows_sum(jnp.where(iota(x.shape, 1) == lane, x, 0.0))


def pick_row(x, sub):
    return jnp.sum(jnp.where(iota(x.shape, 0) == sub, x, 0.0), axis=0, keepdims=True)


def greet(devices):
    barrier = pltpu.get_barrier_semaphore()
    for device in devices:
        pl.semaphore_signal(barrier, inc=1, device_id=device, device_id_type=MESH)
    pl.semaphore_wait(barrier, len(devices))


def ring_pair(count):
    place = lax.axis_index("ctx")
    return [{"ctx": lax.rem(place + 1, count)}, {"ctx": lax.rem(place + count - 1, count)}]


def others(axis, count):
    place = lax.axis_index(axis)
    return [{axis: lax.rem(place + step, count)} for step in range(1, count)]


def halo_kernel(count, q_ref, k_ref, v_ref, halo_ref, land, send_sem, recv_sem):
    place = lax.axis_index("ctx")
    tokens = q_ref.shape[0]
    greet(ring_pair(count))

    def copy(number, ref):
        return pltpu.make_async_remote_copy(
            src_ref=ref.at[pl.ds(tokens - TILE, TILE)],
            dst_ref=land.at[number],
            send_sem=send_sem.at[number],
            recv_sem=recv_sem.at[number],
            device_id={"ctx": lax.rem(place + 1, count)},
            device_id_type=MESH,
        )

    copies = [copy(number, ref) for number, ref in enumerate((q_ref, k_ref, v_ref))]

    @pl.when(place < count - 1)
    def _():
        for one in copies:
            one.start()

    @pl.when(place == 0)
    def _():
        halo_ref[...] = jnp.zeros_like(halo_ref)

    @pl.when(place > 0)
    def _():
        for one in copies:
            one.wait_recv()
        halo_ref[...] = land[...]

    @pl.when(place < count - 1)
    def _():
        for one in copies:
            one.wait_send()


def local_kernel(
    group,
    q_ref,
    k_ref,
    v_ref,
    halo_ref,
    conv_ref,
    decay_ref,
    beta_ref,
    rate_ref,
    reset_ref,
    y_ref,
    query_ref,
    key_ref,
    inv_ref,
    attn_ref,
    reach_key_ref,
    base_ref,
    reach_ref,
    mix_ref,
    carry_p_ref,
    carry_q_ref,
    padded,
):
    step = pl.program_id(0)
    length, width = q_ref.shape
    size = width // group
    taps = conv_ref.shape[1]
    keep = (1 - reset_ref[0, 0]).astype(F32)
    acts = []
    for number, ref in enumerate((q_ref, k_ref, v_ref)):
        padded[0:8, :] = halo_ref[number].astype(F32)[TILE - 8 :] * keep
        padded[8 : 8 + length, :] = ref[...].astype(F32)
        total = conv_ref[number, 0:1, :] * padded[8 : 8 + length, :]
        for tap in range(1, taps):
            total = total + conv_ref[number, tap : tap + 1, :] * padded[8 - tap : 8 - tap + length, :]
        y_ref[number] = total
        acts.append(total * jax.nn.sigmoid(total))
    gate = gates(decay_ref[...], rate_ref[...])[1]
    cumul_col, cumul_row = cumul_forms(gate)
    write_all = jax.nn.sigmoid(beta_ref[...])
    row_i = iota((length, length), 0)
    col_i = iota((length, length), 1)
    eye = (row_i == col_i).astype(F32)
    heads = range(group)
    state = []
    for j in heads:
        head = step * group + j
        cols = slice(j * size, (j + 1) * size)
        act_q, act_k, value = acts[0][:, cols], acts[1][:, cols], acts[2][:, cols]
        query = act_q * lax.rsqrt(rows_sum(act_q * act_q) + EPS) * size ** (-0.5)
        key = act_k * lax.rsqrt(rows_sum(act_k * act_k) + EPS)
        query_ref[j] = query
        key_ref[j] = key
        col = pick_col(cumul_col, head)
        row = pick_row(cumul_row, head)
        write = pick_col(write_all, head)
        spread = jnp.exp(jnp.minimum(col - row, 0.0))
        key_pair = pair(key)
        query_pair = pair(query)
        inner = dot3(key_pair, pair(write * key), NT)
        system = jnp.where(row_i > col_i, spread * inner, 0.0)
        attn = jnp.where(row_i >= col_i, spread * dot3(query_pair, key_pair, NT), 0.0)
        attn_ref[j] = attn
        state.append((key, query, value, col, write, system, attn, key_pair))
    inverse = [
        eye - jnp.where((row_i >> 1) == (col_i >> 1), state[j][5], 0.0) for j in heads
    ]
    level = 1
    while (2 << level) <= length:
        mask = ((row_i >> (level + 1)) == (col_i >> (level + 1))) & (
            (row_i >> level) != (col_i >> level)
        )
        pairs = [pair(inverse[j]) for j in heads]
        middle = [
            dot3(pairs[j], pair(jnp.where(mask, state[j][5], 0.0)), NN) for j in heads
        ]
        inverse = [inverse[j] - dot3(pair(middle[j]), pairs[j], NN) for j in heads]
        level += 1
    for j in heads:
        key, query, value, col, write, system, attn, key_pair = state[j]
        inv_ref[j] = inverse[j]
        inv_pair = pair(inverse[j])
        growth = jnp.exp(col)
        last = col[length - 1 : length, :]
        tail = jnp.exp(last - col)
        base = dot3(inv_pair, pair(value), NN)
        reach_key = dot3(inv_pair, pair(growth * key), NN)
        base_ref[j] = base
        reach_key_ref[j] = reach_key
        attn_pair = pair(attn)
        wide_base = write * base
        wide_reach = write * reach_key
        mix_ref[j] = dot3(attn_pair, pair(wide_base), NN)
        reach_ref[j] = keep * (growth * query - dot3(attn_pair, pair(wide_reach), NN))
        carry_q_ref[j] = dot3(pair(tail * wide_base), key_pair, TN)
        carry_p_ref[j] = keep * (
            jnp.exp(last) * eye - dot3(pair(tail * wide_reach), key_pair, TN)
        )


def chain_kernel(
    count,
    partners,
    mix_ref,
    reach_ref,
    carry_p_ref,
    carry_q_ref,
    d_out_ref,
    gain_ref,
    mixed_ref,
    stat_ref,
    state_ref,
    grad_ref,
    state_land,
    state_out,
    grad_land,
    grad_out,
    stat_land,
    state_send,
    state_recv,
    grad_send,
    grad_recv,
    stat_send,
    stat_recv,
):
    place = lax.axis_index("ctx")
    heads, length, size = mix_ref.shape
    full_width = heads * size * partners
    greet(ring_pair(count) + others("head", partners))

    def state_copy(h):
        return pltpu.make_async_remote_copy(
            src_ref=state_out.at[h],
            dst_ref=state_land.at[h],
            send_sem=state_send.at[h],
            recv_sem=state_recv.at[h],
            device_id={"ctx": lax.rem(place + 1, count)},
            device_id_type=MESH,
        )

    def grad_copy(h):
        return pltpu.make_async_remote_copy(
            src_ref=grad_out.at[h],
            dst_ref=grad_land.at[h],
            send_sem=grad_send.at[h],
            recv_sem=grad_recv.at[h],
            device_id={"ctx": lax.rem(place + count - 1, count)},
            device_id_type=MESH,
        )

    @pl.when(place == 0)
    def _():
        state_ref[...] = jnp.zeros_like(state_ref)

        def first(h, carry):
            state_out[h] = carry_q_ref[h]
            if count > 1:
                state_copy(h).start()
            return carry

        lax.fori_loop(0, heads, first, 0)

    @pl.when(place > 0)
    def _():
        def hop(h, carry):
            state_copy(h).wait_recv()
            entering = state_land[h]
            state_ref[h] = entering

            @pl.when(place < count - 1)
            def _():
                state_out[h] = carry_q_ref[h] + dot3(pair(entering), pair(carry_p_ref[h]), NN)
                state_copy(h).start()

            return carry

        lax.fori_loop(0, heads, hop, 0)

    def mixing(h, carry):
        square, inner = carry
        cols = pl.ds(pl.multiple_of(h * size, size), size)
        mixed = mix_ref[h] + dot3(pair(reach_ref[h]), pair(state_ref[h]), NT)
        mixed_ref[:, cols] = mixed
        weighted = d_out_ref[:, cols].astype(F32) * gain_ref[:, cols]
        return square + mixed * mixed, inner + weighted * mixed

    zero = jnp.zeros((length, size), F32)
    square, inner = lax.fori_loop(0, heads, mixing, (zero, zero))
    half = iota((length, size), 1) < size // 2
    mine = lax.axis_index("head")
    stat_land[mine] = jnp.where(half, rows_sum(square), rows_sum(inner))

    def stat_copy(target, slot):
        return pltpu.make_async_remote_copy(
            src_ref=stat_land.at[mine],
            dst_ref=stat_land.at[slot],
            send_sem=stat_send.at[target],
            recv_sem=stat_recv.at[slot],
            device_id={"head": target},
            device_id_type=MESH,
        )

    for step in range(1, partners):
        stat_copy(lax.rem(mine + step, partners), mine).start()
    for step in range(1, partners):
        source = lax.rem(mine + step, partners)
        stat_copy(source, source).wait_recv()
    stat = stat_land[0]
    for slot in range(1, partners):
        stat = stat + stat_land[slot]
    stat_ref[...] = stat
    scale = lax.rsqrt(stat[:, 0:1] / full_width + EPS)
    coef = scale * scale * scale * stat[:, size - 1 : size] / full_width

    def source_grad(h, carry):
        cols = pl.ds(pl.multiple_of(h * size, size), size)
        weighted = d_out_ref[:, cols].astype(F32) * gain_ref[:, cols]
        grad_mixed = weighted * scale - mixed_ref[:, cols] * coef
        grad_out[h] = dot3(pair(grad_mixed), pair(reach_ref[h]), TN)

        @pl.when((place == count - 1) & (place > 0))
        def _():
            grad_copy(h).start()

        return carry

    @pl.when(place > 0)
    def _():
        lax.fori_loop(0, heads, source_grad, 0)

    @pl.when(place == count - 1)
    def _():
        grad_ref[...] = jnp.zeros_like(grad_ref)

    @pl.when(place < count - 1)
    def _():
        def hop(h, carry):
            grad_copy(h).wait_recv()
            leaving = grad_land[h]
            grad_ref[h] = leaving

            @pl.when(place > 0)
            def _():
                grad_out[h] = grad_out[h] + dot3(pair(leaving), pair(carry_p_ref[h]), NT)
                grad_copy(h).start()

            return carry

        lax.fori_loop(0, heads, hop, 0)

    for step in range(1, partners):
        stat_copy(lax.rem(mine + step, partners), mine).wait_send()

    @pl.when(place < count - 1)
    def _():
        def done(h, carry):
            state_copy(h).wait_send()
            return carry

        lax.fori_loop(0, heads, done, 0)

    @pl.when(place > 0)
    def _():
        def done(h, carry):
            grad_copy(h).wait_send()
            return carry

        lax.fori_loop(0, heads, done, 0)


def back_kernel(
    group,
    full_width,
    q_ref,
    k_ref,
    v_ref,
    halo_ref,
    conv_ref,
    decay_ref,
    beta_ref,
    rate_ref,
    reset_ref,
    d_out_ref,
    gain_ref,
    mixed_ref,
    stat_ref,
    y_ref,
    query_ref,
    key_ref,
    inv_ref,
    attn_ref,
    reach_key_ref,
    base_ref,
    state_ref,
    grad_ref,
    out_ref,
    dq_ref,
    dk_ref,
    dv_ref,
    edge_ref,
    back_ref,
    param_ref,
    d_decay_ref,
    d_beta_ref,
    padded,
    d_conv,
):
    step = pl.program_id(0)
    length, width = q_ref.shape
    size = width // group
    taps = conv_ref.shape[1]
    keep = (1 - reset_ref[0, 0]).astype(F32)
    stat = stat_ref[...]
    scale = lax.rsqrt(stat[:, 0:1] / full_width + EPS)
    coef = scale * scale * scale * stat[:, size - 1 : size] / full_width
    mixed = mixed_ref[...]
    grad_y = d_out_ref[...].astype(F32)
    gain = gain_ref[...]
    normal = mixed * scale
    out_ref[...] = (normal * gain).astype(BF16)
    param_ref[...] = jnp.zeros_like(param_ref)
    param_ref[12:13, :] = jnp.sum(grad_y * normal, axis=0, keepdims=True)
    grad_mixed = grad_y * gain * scale - mixed * coef

    soft, gate = gates(decay_ref[...], rate_ref[...])
    slope = jax.nn.sigmoid(decay_ref[...])
    cumul_col, cumul_row = cumul_forms(gate)
    write_all = jax.nn.sigmoid(beta_ref[...])
    row_i = iota((length, length), 0)
    col_i = iota((length, length), 1)
    upper = (row_i <= col_i).astype(F32).astype(BF16)
    lanes = iota(decay_ref.shape, 1)

    @pl.when(step == 0)
    def _():
        d_decay_ref[...] = jnp.zeros_like(d_decay_ref)
        d_beta_ref[...] = jnp.zeros_like(d_beta_ref)

    heads = range(group)
    pre = []
    for j in heads:
        cols = slice(j * size, (j + 1) * size)
        head = step * group + j
        col = pick_col(cumul_col, head)
        row = pick_row(cumul_row, head)
        write = pick_col(write_all, head)
        spread = jnp.exp(jnp.minimum(col - row, 0.0))
        growth = jnp.exp(col)
        last = col[length - 1 : length, :]
        tail = jnp.exp(last - col)
        query, key = query_ref[j], key_ref[j]
        entering = keep * state_ref[j]
        leaving = grad_ref[j]
        enter_pair, leave_pair = pair(entering), pair(leaving)
        key_pair, query_pair = pair(key), pair(query)
        grad = grad_mixed[:, cols]
        grad_pair = pair(grad)
        delta = base_ref[j] - dot3(pair(reach_key_ref[j]), enter_pair, NT)
        used = write * delta
        used_pair = pair(used)
        d_used = dot3(pair(attn_ref[j]), grad_pair, TN) + tail * dot3(key_pair, leave_pair, NT)
        d_attn = jnp.where(row_i >= col_i, spread * dot3(grad_pair, used_pair, NT), 0.0)
        d_attn_pair = pair(d_attn)
        d_query = growth * dot3(grad_pair, enter_pair, NN) + dot3(d_attn_pair, key_pair, NN)
        d_key_tail = tail * dot3(used_pair, leave_pair, NN)
        d_key_plus = dot3(d_attn_pair, query_pair, TN) + d_key_tail
        right = dot3(pair(inv_ref[j]), pair(write * d_used), TN)
        right_pair = pair(right)
        d_system = jnp.where(row_i > col_i, -spread * dot3(right_pair, pair(delta), NT), 0.0)
        d_system_pair = pair(d_system)
        d_inner = dot3(d_system_pair, key_pair, TN)
        d_key_minus = dot3(d_system_pair, pair(write * key), NN) - growth * dot3(
            right_pair, enter_pair, NN
        )
        d_key_plus = d_key_plus + write * d_inner
        d_write = rows_sum(d_used * delta + key * d_inner)
        whole = jnp.sum(rows_sum(key * d_key_tail), axis=0, keepdims=True) + jnp.exp(
            last
        ) * jnp.sum(rows_sum(leaving * entering), axis=0, keepdims=True)
        d_cumul = rows_sum(query * d_query + key * (d_key_minus - d_key_plus))
        spot = jnp.where(iota(d_cumul.shape, 0) == length - 1, whole, 0.0)
        d_cumul = jnp.broadcast_to(d_cumul + spot, (length, size))
        d_gate = sum(dot_dims(upper, p, NN) for p in pair(d_cumul))[:, 0:1]
        d_key = d_key_plus + d_key_minus
        here = lanes == head
        d_decay_ref[...] += jnp.where(here, -rate_ref[...] * slope * d_gate, 0.0)
        d_beta_ref[...] += jnp.where(here, d_write * write_all * (1.0 - write_all), 0.0)
        d_rate = -jnp.sum(jnp.where(here, soft * d_gate, 0.0), keepdims=True)
        param_ref[13:14, cols] = jnp.broadcast_to(d_rate, (1, size))
        pre.append((d_query, d_key, right))

    rooted = size ** (-0.5)
    back_ref[...] = jnp.zeros_like(back_ref)
    for number, (ref, dst) in enumerate(((q_ref, dq_ref), (k_ref, dk_ref), (v_ref, dv_ref))):
        d_conv[0:8, :] = jnp.zeros((8, width), F32)
        d_conv[8 + length :, :] = jnp.zeros((8, width), F32)
        padded[0:8, :] = halo_ref[number].astype(F32)[TILE - 8 :] * keep
        padded[8 : 8 + length, :] = ref[...].astype(F32)
        for j in heads:
            cols = slice(j * size, (j + 1) * size)
            total = y_ref[number, :, cols]
            gated = jax.nn.sigmoid(total)
            grad = pre[j][number]
            if number < 2:
                act = total * gated
                inv_norm = lax.rsqrt(rows_sum(act * act) + EPS)
                unit = act * inv_norm
                if number == 0:
                    grad = grad * rooted
                grad = inv_norm * (grad - unit * rows_sum(unit * grad))
            d_conv[8 : 8 + length, cols] = grad * (gated * (1.0 + total * (1.0 - gated)))
        grad = d_conv[8 : 8 + length, :]
        extended = conv_ref[number, 0:1, :] * d_conv[0 : 8 + length, :]
        param_ref[4 * number : 4 * number + 1, :] = jnp.sum(
            grad * padded[8 : 8 + length, :], axis=0, keepdims=True
        )
        for tap in range(1, taps):
            extended = extended + conv_ref[number, tap : tap + 1, :] * d_conv[tap : tap + 8 + length, :]
            param_ref[4 * number + tap : 4 * number + tap + 1, :] = jnp.sum(
                grad * padded[8 - tap : 8 - tap + length, :], axis=0, keepdims=True
            )
        dst[...] = extended[8:].astype(BF16)
        edge_ref[8 * number : 8 * number + 8, :] = extended[length:]
        back_ref[8 * number : 8 * number + 8, :] = (keep * extended[0:8]).astype(BF16)


def sum_kernel(
    count,
    pairs,
    param_ref,
    back_ref,
    total_ref,
    arrived_ref,
    near_land,
    far_land,
    final_land,
    back_land,
    near_send,
    near_recv,
    far_send,
    far_recv,
    final_send,
    final_recv,
    back_send,
    back_recv,
):
    place = lax.axis_index("ctx")
    mine = lax.axis_index("dp")
    greet(others("ctx", count) + others("dp", pairs))

    back = pltpu.make_async_remote_copy(
        src_ref=back_ref,
        dst_ref=back_land,
        send_sem=back_send,
        recv_sem=back_recv,
        device_id={"ctx": lax.rem(place + count - 1, count)},
        device_id_type=MESH,
    )

    @pl.when(place > 0)
    def _():
        back.start()

    def near(target, slot):
        return pltpu.make_async_remote_copy(
            src_ref=param_ref.at[target],
            dst_ref=near_land.at[slot],
            send_sem=near_send.at[target],
            recv_sem=near_recv.at[slot],
            device_id={"dp": target},
            device_id_type=MESH,
        )

    def far(target, slot):
        return pltpu.make_async_remote_copy(
            src_ref=far_land.at[place],
            dst_ref=far_land.at[slot],
            send_sem=far_send.at[target],
            recv_sem=far_recv.at[slot],
            device_id={"ctx": target},
            device_id_type=MESH,
        )

    def final(target, slot):
        return pltpu.make_async_remote_copy(
            src_ref=final_land.at[mine],
            dst_ref=final_land.at[slot],
            send_sem=final_send.at[target],
            recv_sem=final_recv.at[slot],
            device_id={"dp": target},
            device_id_type=MESH,
        )

    def exchange(copy, here, total):
        for step in range(1, total):
            copy(lax.rem(here + step, total), here).start()
        for step in range(1, total):
            source = lax.rem(here + step, total)
            copy(source, source).wait_recv()

    def settle(copy, here, total):
        for step in range(1, total):
            copy(lax.rem(here + step, total), here).wait_send()

    near_land[mine] = param_ref[mine]
    exchange(near, mine, pairs)
    part = near_land[0]
    for slot in range(1, pairs):
        part = part + near_land[slot]
    far_land[place] = part
    exchange(far, place, count)
    part = far_land[0]
    for slot in range(1, count):
        part = part + far_land[slot]
    final_land[mine] = part
    exchange(final, mine, pairs)
    total_ref[...] = final_land[...]

    @pl.when(place == count - 1)
    def _():
        arrived_ref[...] = jnp.zeros_like(arrived_ref)

    @pl.when(place < count - 1)
    def _():
        back.wait_recv()
        arrived_ref[...] = back_land[...]

    settle(near, mine, pairs)
    settle(far, place, count)
    settle(final, mine, pairs)

    @pl.when(place > 0)
    def _():
        back.wait_send()


def remote_params(number):
    return pltpu.CompilerParams(
        collective_id=number, has_side_effects=True, vmem_limit_bytes=VMEM_BYTES
    )


def body(
    q_raw,
    k_raw,
    v_raw,
    conv_weight,
    decay_logit,
    beta_logit,
    decay_rate,
    block_resets,
    norm_gain,
    d_out,
):
    tokens, width = q_raw.shape[1:]
    heads = decay_logit.shape[2]
    size = width // heads
    taps = conv_weight.shape[1]
    count = lax.axis_size("ctx")
    partners = lax.axis_size("head")
    pairs = lax.axis_size("dp")
    group = 4 if heads % 4 == 0 else 1
    steps = heads // group
    span = group * size
    vmem = pl.BlockSpec(memory_space=pltpu.VMEM)
    shape = jax.ShapeDtypeStruct
    dma = pltpu.SemaphoreType.DMA
    raws = (q_raw[0], k_raw[0], v_raw[0])
    gain = norm_gain[None, :]
    rate = decay_rate[None, :]
    decay, beta = decay_logit[0], beta_logit[0]

    halo = pl.pallas_call(
        functools.partial(halo_kernel, count),
        out_shape=shape((3, TILE, width), BF16),
        in_specs=[pl.BlockSpec(memory_space=pl.ANY)] * 3,
        out_specs=vmem,
        scratch_shapes=[pltpu.VMEM((3, TILE, width), BF16), dma((3,)), dma((3,))],
        compiler_params=remote_params(0),
        name="halo",
    )(*raws)

    cols = pl.BlockSpec((tokens, span), lambda i: (0, i))
    halo_cols = pl.BlockSpec((3, TILE, span), lambda i: (0, 0, i))
    conv_cols = pl.BlockSpec((3, taps, span), lambda i: (0, 0, i))
    y_cols = pl.BlockSpec((3, tokens, span), lambda i: (0, 0, i))
    gate_all = pl.BlockSpec((tokens, heads), lambda i: (0, 0))
    rate_all = pl.BlockSpec((1, heads), lambda i: (0, 0))
    flag = pl.BlockSpec(memory_space=pltpu.SMEM)
    square = pl.BlockSpec((group, tokens, size), lambda i: (i, 0, 0))
    matrix = shape((heads, tokens, size), F32)
    local = pl.pallas_call(
        functools.partial(local_kernel, group),
        grid=(steps,),
        out_shape=[shape((3, tokens, width), F32)] + [matrix] * 10,
        in_specs=[cols] * 3 + [halo_cols, conv_cols, gate_all, gate_all, rate_all, flag],
        out_specs=[y_cols] + [square] * 10,
        scratch_shapes=[pltpu.VMEM((tokens + 8, span), F32)],
        compiler_params=pltpu.CompilerParams(vmem_limit_bytes=VMEM_BYTES),
        name="local",
    )(*raws, halo, conv_weight, decay, beta, rate, block_resets)
    y, query, key, inverse, attn, reach_key, base, reach, mix, carry_p, carry_q = local

    buffer = pltpu.VMEM((heads, size, size), F32)
    mixed, stat, state, grad = pl.pallas_call(
        functools.partial(chain_kernel, count, partners),
        out_shape=[
            shape((tokens, width), F32),
            shape((tokens, size), F32),
            shape((heads, size, size), F32),
            shape((heads, size, size), F32),
        ],
        in_specs=[vmem] * 6,
        out_specs=[vmem] * 4,
        scratch_shapes=[buffer] * 4
        + [pltpu.VMEM((partners, tokens, size), F32)]
        + [dma((heads,))] * 4
        + [dma((partners,))] * 2,
        compiler_params=remote_params(1),
        name="chain",
    )(mix, reach, carry_p, carry_q, d_out[0], gain)

    gain_cols = pl.BlockSpec((1, span), lambda i: (0, i))
    stat_all = pl.BlockSpec((tokens, size), lambda i: (0, 0))
    rows = lambda n: pl.BlockSpec((n, span), lambda i: (0, i))
    wide = shape((tokens, width), BF16)
    out, d_q, d_k, d_v, edge, back, param, d_decay, d_beta = pl.pallas_call(
        functools.partial(back_kernel, group, width * partners),
        grid=(steps,),
        out_shape=[wide] * 4
        + [
            shape((24, width), F32),
            shape((32, width), BF16),
            shape((16, width), F32),
            shape((tokens, heads), F32),
            shape((tokens, heads), F32),
        ],
        in_specs=[cols] * 3
        + [halo_cols, conv_cols, gate_all, gate_all, rate_all, flag]
        + [cols, gain_cols, cols, stat_all, y_cols]
        + [square] * 8,
        out_specs=[cols] * 4 + [rows(24), rows(32), rows(16), gate_all, gate_all],
        scratch_shapes=[
            pltpu.VMEM((tokens + 8, span), F32),
            pltpu.VMEM((tokens + 16, span), F32),
        ],
        compiler_params=pltpu.CompilerParams(vmem_limit_bytes=VMEM_BYTES),
        name="back",
    )(
        *raws, halo, conv_weight, decay, beta, rate, block_resets, d_out[0], gain, mixed, stat,
        y, query, key, inverse, attn, reach_key, base, state, grad,
    )

    rows_each = 16 // pairs
    total, arrived = pl.pallas_call(
        functools.partial(sum_kernel, count, pairs),
        out_shape=[shape((pairs, rows_each, width), F32), shape((32, width), BF16)],
        in_specs=[vmem] * 2,
        out_specs=[vmem] * 2,
        scratch_shapes=[
            pltpu.VMEM((pairs, rows_each, width), F32),
            pltpu.VMEM((count, rows_each, width), F32),
            pltpu.VMEM((pairs, rows_each, width), F32),
            pltpu.VMEM((32, width), BF16),
            dma((pairs,)),
            dma((pairs,)),
            dma((count,)),
            dma((count,)),
            dma((pairs,)),
            dma((pairs,)),
            dma,
            dma,
        ],
        compiler_params=remote_params(2),
        name="sums",
    )(param.reshape(pairs, rows_each, width), back)
    total = total.reshape(16, width)
    borrowed = taps - 1

    def finish(number, whole):
        come = arrived[8 * number + 8 - borrowed : 8 * number + 8].astype(F32)
        rows = (edge[8 * number + 8 - borrowed : 8 * number + 8] + come).astype(BF16)
        return lax.dynamic_update_slice(whole, rows, (tokens - borrowed, 0))[None]

    return (
        out[None],
        finish(0, d_q),
        finish(1, d_k),
        finish(2, d_v),
        total[:12].reshape(3, taps, width),
        d_decay[None],
        d_beta[None],
        total[13].reshape(heads, size)[:, 0],
        total[12],
    )


def solution(mesh):
    placed = (
        P("dp", "ctx", "head"),
        P("dp", "ctx", "head"),
        P("dp", "ctx", "head"),
        P(None, None, "head"),
        P("dp", "ctx", "head"),
        P("dp", "ctx", "head"),
        P("head"),
        P("dp", "ctx"),
        P("head"),
        P("dp", "ctx", "head"),
    )
    return jax.shard_map(
        body,
        mesh=mesh,
        in_specs=placed,
        out_specs=(
            P("dp", "ctx", "head"),
            P("dp", "ctx", "head"),
            P("dp", "ctx", "head"),
            P("dp", "ctx", "head"),
            P(None, None, "head"),
            P("dp", "ctx", "head"),
            P("dp", "ctx", "head"),
            P("head"),
            P("head"),
        ),
        check_vma=False,
    )
```

```python
import functools

import jax
import jax.numpy as jnp
from jax import lax
from jax.experimental import pallas as pl
from jax.experimental.pallas import tpu as pltpu
from jax.sharding import PartitionSpec as P

F32 = jnp.float32
BF16 = jnp.bfloat16
MESH = pl.DeviceIdType.MESH
VMEM_BYTES = 56 * 1024 * 1024
TILE = 16
EPS = 1e-06


def pair(x):
    hi = x.astype(BF16)
    return hi, (x - hi.astype(F32)).astype(BF16)


def dot_dims(a, b, dims):
    return lax.dot_general(a, b, (dims, ((), ())), preferred_element_type=F32)


def dot3(a, b, dims):
    return dot_dims(a[0], b[0], dims) + (dot_dims(a[0], b[1], dims) + dot_dims(a[1], b[0], dims))


NN = ((1,), (0,))
NT = ((1,), (1,))
TN = ((0,), (0,))


def iota(shape, dim):
    return lax.broadcasted_iota(jnp.int32, shape, dim)


def rows_sum(x):
    return jnp.sum(x, axis=1, keepdims=True)


def gates(logit, rate):
    soft = jnp.maximum(logit, 0.0) + jnp.log1p(jnp.exp(-jnp.abs(logit)))
    return soft, -rate * soft


def triple(x):
    hi, rest = pair(x)
    lo = (x - hi.astype(F32) - rest.astype(F32)).astype(BF16)
    return hi, rest, lo


def cumul_forms(gate):
    length = gate.shape[1]
    lower = (iota((length, length), 0) >= iota((length, length), 1)).astype(F32).astype(BF16)
    parts = triple(gate)
    col = sum(dot_dims(lower, p, NT) for p in parts)
    row = sum(dot_dims(p, lower, NT) for p in parts)
    return col, row


def pick_col(x, lane):
    return rows_sum(jnp.where(iota(x.shape, 1) == lane, x, 0.0))


def pick_row(x, sub):
    return jnp.sum(jnp.where(iota(x.shape, 0) == sub, x, 0.0), axis=0, keepdims=True)


def column(row):
    shape = (row.shape[1], row.shape[1])
    spot = iota(shape, 0) == iota(shape, 1)
    return rows_sum(jnp.where(spot, jnp.broadcast_to(row, shape), 0.0))


def greet(devices):
    barrier = pltpu.get_barrier_semaphore()
    for device in devices:
        pl.semaphore_signal(barrier, inc=1, device_id=device, device_id_type=MESH)
    pl.semaphore_wait(barrier, len(devices))


def ring_pair(count):
    place = lax.axis_index("ctx")
    return [{"ctx": lax.rem(place + 1, count)}, {"ctx": lax.rem(place + count - 1, count)}]


def others(axis, count):
    place = lax.axis_index(axis)
    return [{axis: lax.rem(place + step, count)} for step in range(1, count)]


def halo_kernel(count, q_ref, k_ref, v_ref, halo_ref, land, send_sem, recv_sem):
    place = lax.axis_index("ctx")
    tokens = q_ref.shape[0]
    greet(ring_pair(count))

    def copy(number, ref):
        return pltpu.make_async_remote_copy(
            src_ref=ref.at[pl.ds(tokens - TILE, TILE)],
            dst_ref=land.at[number],
            send_sem=send_sem.at[number],
            recv_sem=recv_sem.at[number],
            device_id={"ctx": lax.rem(place + 1, count)},
            device_id_type=MESH,
        )

    copies = [copy(number, ref) for number, ref in enumerate((q_ref, k_ref, v_ref))]

    @pl.when(place < count - 1)
    def _():
        for one in copies:
            one.start()

    @pl.when(place == 0)
    def _():
        halo_ref[...] = jnp.zeros_like(halo_ref)

    @pl.when(place > 0)
    def _():
        for one in copies:
            one.wait_recv()
        halo_ref[...] = land[...]

    @pl.when(place < count - 1)
    def _():
        for one in copies:
            one.wait_send()


def local_kernel(
    group,
    q_ref,
    k_ref,
    v_ref,
    halo_ref,
    conv_ref,
    decay_ref,
    beta_ref,
    rate_ref,
    reset_ref,
    y_ref,
    query_ref,
    key_ref,
    inv_ref,
    attn_ref,
    reach_key_ref,
    base_ref,
    reach_ref,
    mix_ref,
    carry_p_ref,
    carry_q_ref,
    padded,
):
    step = pl.program_id(0)
    length, width = q_ref.shape
    size = width // group
    taps = conv_ref.shape[1]
    keep = (1 - reset_ref[0, 0]).astype(F32)
    acts = []
    for number, ref in enumerate((q_ref, k_ref, v_ref)):
        padded[0:8, :] = halo_ref[number].astype(F32)[TILE - 8 :] * keep
        padded[8 : 8 + length, :] = ref[...].astype(F32)
        total = conv_ref[number, 0:1, :] * padded[8 : 8 + length, :]
        for tap in range(1, taps):
            total = total + conv_ref[number, tap : tap + 1, :] * padded[8 - tap : 8 - tap + length, :]
        y_ref[number] = total
        acts.append(total * jax.nn.sigmoid(total))
    gate = gates(decay_ref[...], column(rate_ref[...]))[1]
    cumul_col, cumul_row = cumul_forms(gate)
    write_all = jax.nn.sigmoid(beta_ref[...])
    row_i = iota((length, length), 0)
    col_i = iota((length, length), 1)
    eye = (row_i == col_i).astype(F32)
    heads = range(group)
    state = []
    for j in heads:
        head = step * group + j
        cols = slice(j * size, (j + 1) * size)
        act_q, act_k, value = acts[0][:, cols], acts[1][:, cols], acts[2][:, cols]
        query = act_q * lax.rsqrt(rows_sum(act_q * act_q) + EPS) * size ** (-0.5)
        key = act_k * lax.rsqrt(rows_sum(act_k * act_k) + EPS)
        query_ref[j] = query
        key_ref[j] = key
        col = pick_col(cumul_col, head)
        row = pick_row(cumul_row, head)
        write = column(pick_row(write_all, head))
        spread = jnp.exp(jnp.minimum(col - row, 0.0))
        key_pair = pair(key)
        query_pair = pair(query)
        inner = dot3(key_pair, pair(write * key), NT)
        system = jnp.where(row_i > col_i, spread * inner, 0.0)
        attn = jnp.where(row_i >= col_i, spread * dot3(query_pair, key_pair, NT), 0.0)
        attn_ref[j] = attn
        state.append((key, query, value, col, write, system, attn, key_pair))
    inverse = [
        eye - jnp.where((row_i >> 1) == (col_i >> 1), state[j][5], 0.0) for j in heads
    ]
    level = 1
    while (2 << level) <= length:
        mask = ((row_i >> (level + 1)) == (col_i >> (level + 1))) & (
            (row_i >> level) != (col_i >> level)
        )
        pairs = [pair(inverse[j]) for j in heads]
        middle = [
            dot3(pairs[j], pair(jnp.where(mask, state[j][5], 0.0)), NN) for j in heads
        ]
        inverse = [inverse[j] - dot3(pair(middle[j]), pairs[j], NN) for j in heads]
        level += 1
    for j in heads:
        key, query, value, col, write, system, attn, key_pair = state[j]
        inv_ref[j] = inverse[j]
        inv_pair = pair(inverse[j])
        growth = jnp.exp(col)
        last = col[length - 1 : length, :]
        tail = jnp.exp(last - col)
        base = dot3(inv_pair, pair(value), NN)
        reach_key = dot3(inv_pair, pair(growth * key), NN)
        base_ref[j] = base
        reach_key_ref[j] = reach_key
        attn_pair = pair(attn)
        wide_base = write * base
        wide_reach = write * reach_key
        mix_ref[j] = dot3(attn_pair, pair(wide_base), NN)
        reach_ref[j] = keep * (growth * query - dot3(attn_pair, pair(wide_reach), NN))
        carry_q_ref[j] = dot3(pair(tail * wide_base), key_pair, TN)
        carry_p_ref[j] = keep * (
            jnp.exp(last) * eye - dot3(pair(tail * wide_reach), key_pair, TN)
        )


def chain_kernel(
    count,
    partners,
    mix_ref,
    reach_ref,
    carry_p_ref,
    carry_q_ref,
    d_out_ref,
    gain_ref,
    mixed_ref,
    stat_ref,
    state_ref,
    grad_ref,
    state_land,
    state_out,
    grad_land,
    grad_out,
    stat_land,
    state_send,
    state_recv,
    grad_send,
    grad_recv,
    stat_send,
    stat_recv,
):
    place = lax.axis_index("ctx")
    heads, length, size = mix_ref.shape
    full_width = heads * size * partners
    greet(ring_pair(count) + others("head", partners))

    def state_copy(h):
        return pltpu.make_async_remote_copy(
            src_ref=state_out.at[h],
            dst_ref=state_land.at[h],
            send_sem=state_send.at[h],
            recv_sem=state_recv.at[h],
            device_id={"ctx": lax.rem(place + 1, count)},
            device_id_type=MESH,
        )

    def grad_copy(h):
        return pltpu.make_async_remote_copy(
            src_ref=grad_out.at[h],
            dst_ref=grad_land.at[h],
            send_sem=grad_send.at[h],
            recv_sem=grad_recv.at[h],
            device_id={"ctx": lax.rem(place + count - 1, count)},
            device_id_type=MESH,
        )

    @pl.when(place == 0)
    def _():
        state_ref[...] = jnp.zeros_like(state_ref)

        def first(h, carry):
            state_out[h] = carry_q_ref[h]
            if count > 1:
                state_copy(h).start()
            return carry

        lax.fori_loop(0, heads, first, 0)

    @pl.when(place > 0)
    def _():
        def hop(h, carry):
            state_copy(h).wait_recv()
            entering = state_land[h]
            state_ref[h] = entering

            @pl.when(place < count - 1)
            def _():
                state_out[h] = carry_q_ref[h] + dot3(pair(entering), pair(carry_p_ref[h]), NN)
                state_copy(h).start()

            return carry

        lax.fori_loop(0, heads, hop, 0)

    def mixing(h, carry):
        square, inner = carry
        cols = pl.ds(pl.multiple_of(h * size, size), size)
        mixed = mix_ref[h] + dot3(pair(reach_ref[h]), pair(state_ref[h]), NT)
        mixed_ref[:, cols] = mixed
        weighted = d_out_ref[:, cols].astype(F32) * gain_ref[:, cols]
        return square + mixed * mixed, inner + weighted * mixed

    zero = jnp.zeros((length, size), F32)
    square, inner = lax.fori_loop(0, heads, mixing, (zero, zero))
    half = iota((length, size), 1) < size // 2
    mine = lax.axis_index("head")
    stat_land[mine] = jnp.where(half, rows_sum(square), rows_sum(inner))

    def stat_copy(target, slot):
        return pltpu.make_async_remote_copy(
            src_ref=stat_land.at[mine],
            dst_ref=stat_land.at[slot],
            send_sem=stat_send.at[target],
            recv_sem=stat_recv.at[slot],
            device_id={"head": target},
            device_id_type=MESH,
        )

    for step in range(1, partners):
        stat_copy(lax.rem(mine + step, partners), mine).start()
    for step in range(1, partners):
        source = lax.rem(mine + step, partners)
        stat_copy(source, source).wait_recv()
    stat = stat_land[0]
    for slot in range(1, partners):
        stat = stat + stat_land[slot]
    stat_ref[...] = stat
    scale = lax.rsqrt(stat[:, 0:1] / full_width + EPS)
    coef = scale * scale * scale * stat[:, size - 1 : size] / full_width

    def source_grad(h, carry):
        cols = pl.ds(pl.multiple_of(h * size, size), size)
        weighted = d_out_ref[:, cols].astype(F32) * gain_ref[:, cols]
        grad_mixed = weighted * scale - mixed_ref[:, cols] * coef
        grad_out[h] = dot3(pair(grad_mixed), pair(reach_ref[h]), TN)

        @pl.when((place == count - 1) & (place > 0))
        def _():
            grad_copy(h).start()

        return carry

    @pl.when(place > 0)
    def _():
        lax.fori_loop(0, heads, source_grad, 0)

    @pl.when(place == count - 1)
    def _():
        grad_ref[...] = jnp.zeros_like(grad_ref)

    @pl.when(place < count - 1)
    def _():
        def hop(h, carry):
            grad_copy(h).wait_recv()
            leaving = grad_land[h]
            grad_ref[h] = leaving

            @pl.when(place > 0)
            def _():
                grad_out[h] = grad_out[h] + dot3(pair(leaving), pair(carry_p_ref[h]), NT)
                grad_copy(h).start()

            return carry

        lax.fori_loop(0, heads, hop, 0)

    for step in range(1, partners):
        stat_copy(lax.rem(mine + step, partners), mine).wait_send()

    @pl.when(place < count - 1)
    def _():
        def done(h, carry):
            state_copy(h).wait_send()
            return carry

        lax.fori_loop(0, heads, done, 0)

    @pl.when(place > 0)
    def _():
        def done(h, carry):
            grad_copy(h).wait_send()
            return carry

        lax.fori_loop(0, heads, done, 0)


def back_kernel(
    group,
    full_width,
    q_ref,
    k_ref,
    v_ref,
    halo_ref,
    conv_ref,
    decay_ref,
    beta_ref,
    rate_ref,
    reset_ref,
    d_out_ref,
    gain_ref,
    mixed_ref,
    stat_ref,
    y_ref,
    query_ref,
    key_ref,
    inv_ref,
    attn_ref,
    reach_key_ref,
    base_ref,
    state_ref,
    grad_ref,
    out_ref,
    dq_ref,
    dk_ref,
    dv_ref,
    edge_ref,
    back_ref,
    param_ref,
    d_decay_ref,
    d_beta_ref,
    padded,
    d_conv,
):
    step = pl.program_id(0)
    length, width = q_ref.shape
    size = width // group
    taps = conv_ref.shape[1]
    keep = (1 - reset_ref[0, 0]).astype(F32)
    stat = stat_ref[...]
    scale = lax.rsqrt(stat[:, 0:1] / full_width + EPS)
    coef = scale * scale * scale * stat[:, size - 1 : size] / full_width
    mixed = mixed_ref[...]
    grad_y = d_out_ref[...].astype(F32)
    gain = gain_ref[...]
    normal = mixed * scale
    out_ref[...] = (normal * gain).astype(BF16)
    param_ref[...] = jnp.zeros_like(param_ref)
    param_ref[12:13, :] = jnp.sum(grad_y * normal, axis=0, keepdims=True)
    grad_mixed = grad_y * gain * scale - mixed * coef

    rate = column(rate_ref[...])
    soft, gate = gates(decay_ref[...], rate)
    slope = jax.nn.sigmoid(decay_ref[...])
    cumul_col, cumul_row = cumul_forms(gate)
    write_all = jax.nn.sigmoid(beta_ref[...])
    row_i = iota((length, length), 0)
    col_i = iota((length, length), 1)
    upper = (row_i <= col_i).astype(F32).astype(BF16)
    gathered = jnp.zeros((length, size), F32)
    half = size // 2

    @pl.when(step == 0)
    def _():
        d_decay_ref[...] = jnp.zeros_like(d_decay_ref)
        d_beta_ref[...] = jnp.zeros_like(d_beta_ref)

    heads = range(group)
    pre = []
    for j in heads:
        cols = slice(j * size, (j + 1) * size)
        head = step * group + j
        col = pick_col(cumul_col, head)
        row = pick_row(cumul_row, head)
        write = column(pick_row(write_all, head))
        spread = jnp.exp(jnp.minimum(col - row, 0.0))
        growth = jnp.exp(col)
        last = col[length - 1 : length, :]
        tail = jnp.exp(last - col)
        query, key = query_ref[j], key_ref[j]
        entering = keep * state_ref[j]
        leaving = grad_ref[j]
        enter_pair, leave_pair = pair(entering), pair(leaving)
        key_pair, query_pair = pair(key), pair(query)
        grad = grad_mixed[:, cols]
        grad_pair = pair(grad)
        delta = base_ref[j] - dot3(pair(reach_key_ref[j]), enter_pair, NT)
        used = write * delta
        used_pair = pair(used)
        d_used = dot3(pair(attn_ref[j]), grad_pair, TN) + tail * dot3(key_pair, leave_pair, NT)
        d_attn = jnp.where(row_i >= col_i, spread * dot3(grad_pair, used_pair, NT), 0.0)
        d_attn_pair = pair(d_attn)
        d_query = growth * dot3(grad_pair, enter_pair, NN) + dot3(d_attn_pair, key_pair, NN)
        d_key_tail = tail * dot3(used_pair, leave_pair, NN)
        d_key_plus = dot3(d_attn_pair, query_pair, TN) + d_key_tail
        right = dot3(pair(inv_ref[j]), pair(write * d_used), TN)
        right_pair = pair(right)
        d_system = jnp.where(row_i > col_i, -spread * dot3(right_pair, pair(delta), NT), 0.0)
        d_system_pair = pair(d_system)
        d_inner = dot3(d_system_pair, key_pair, TN)
        d_key_minus = dot3(d_system_pair, pair(write * key), NN) - growth * dot3(
            right_pair, enter_pair, NN
        )
        d_key_plus = d_key_plus + write * d_inner
        d_write = rows_sum(d_used * delta + key * d_inner)
        whole = jnp.sum(rows_sum(key * d_key_tail), axis=0, keepdims=True) + jnp.exp(
            last
        ) * jnp.sum(rows_sum(leaving * entering), axis=0, keepdims=True)
        d_cumul = rows_sum(query * d_query + key * (d_key_minus - d_key_plus))
        spot = jnp.where(iota(d_cumul.shape, 0) == length - 1, whole, 0.0)
        d_key = d_key_plus + d_key_minus
        gathered = gathered + jnp.where(col_i == head, d_cumul + spot, 0.0)
        gathered = gathered + jnp.where(col_i == half + head, d_write, 0.0)
        pre.append((d_query, d_key, right))

    turned = gathered.T
    count = decay_ref.shape[0]
    d_gate = sum(dot_dims(p, upper, NT) for p in pair(turned[0:count]))
    d_decay_ref[...] += -rate * slope * d_gate
    d_beta_ref[...] += turned[half : half + count] * write_all * (1.0 - write_all)
    d_rate = -rows_sum(soft * d_gate)
    for j in heads:
        one = pick_row(d_rate, step * group + j)
        param_ref[13:14, j * size : (j + 1) * size] = jnp.broadcast_to(one, (1, size))

    rooted = size ** (-0.5)
    back_ref[...] = jnp.zeros_like(back_ref)
    for number, (ref, dst) in enumerate(((q_ref, dq_ref), (k_ref, dk_ref), (v_ref, dv_ref))):
        d_conv[0:8, :] = jnp.zeros((8, width), F32)
        d_conv[8 + length :, :] = jnp.zeros((8, width), F32)
        padded[0:8, :] = halo_ref[number].astype(F32)[TILE - 8 :] * keep
        padded[8 : 8 + length, :] = ref[...].astype(F32)
        for j in heads:
            cols = slice(j * size, (j + 1) * size)
            total = y_ref[number, :, cols]
            gated = jax.nn.sigmoid(total)
            grad = pre[j][number]
            if number < 2:
                act = total * gated
                inv_norm = lax.rsqrt(rows_sum(act * act) + EPS)
                unit = act * inv_norm
                if number == 0:
                    grad = grad * rooted
                grad = inv_norm * (grad - unit * rows_sum(unit * grad))
            d_conv[8 : 8 + length, cols] = grad * (gated * (1.0 + total * (1.0 - gated)))
        grad = d_conv[8 : 8 + length, :]
        extended = conv_ref[number, 0:1, :] * d_conv[0 : 8 + length, :]
        param_ref[4 * number : 4 * number + 1, :] = jnp.sum(
            grad * padded[8 : 8 + length, :], axis=0, keepdims=True
        )
        for tap in range(1, taps):
            extended = extended + conv_ref[number, tap : tap + 1, :] * d_conv[tap : tap + 8 + length, :]
            param_ref[4 * number + tap : 4 * number + tap + 1, :] = jnp.sum(
                grad * padded[8 - tap : 8 - tap + length, :], axis=0, keepdims=True
            )
        dst[...] = extended[8:].astype(BF16)
        edge_ref[8 * number : 8 * number + 8, :] = extended[length:]
        back_ref[8 * number : 8 * number + 8, :] = (keep * extended[0:8]).astype(BF16)


def sum_kernel(
    count,
    pairs,
    param_ref,
    back_ref,
    total_ref,
    arrived_ref,
    near_land,
    far_land,
    final_land,
    back_land,
    near_send,
    near_recv,
    far_send,
    far_recv,
    final_send,
    final_recv,
    back_send,
    back_recv,
):
    place = lax.axis_index("ctx")
    mine = lax.axis_index("dp")
    greet(others("ctx", count) + others("dp", pairs))

    back = pltpu.make_async_remote_copy(
        src_ref=back_ref,
        dst_ref=back_land,
        send_sem=back_send,
        recv_sem=back_recv,
        device_id={"ctx": lax.rem(place + count - 1, count)},
        device_id_type=MESH,
    )

    @pl.when(place > 0)
    def _():
        back.start()

    def near(target, slot):
        return pltpu.make_async_remote_copy(
            src_ref=param_ref.at[target],
            dst_ref=near_land.at[slot],
            send_sem=near_send.at[target],
            recv_sem=near_recv.at[slot],
            device_id={"dp": target},
            device_id_type=MESH,
        )

    def far(target, slot):
        return pltpu.make_async_remote_copy(
            src_ref=far_land.at[place],
            dst_ref=far_land.at[slot],
            send_sem=far_send.at[target],
            recv_sem=far_recv.at[slot],
            device_id={"ctx": target},
            device_id_type=MESH,
        )

    def final(target, slot):
        return pltpu.make_async_remote_copy(
            src_ref=final_land.at[mine],
            dst_ref=final_land.at[slot],
            send_sem=final_send.at[target],
            recv_sem=final_recv.at[slot],
            device_id={"dp": target},
            device_id_type=MESH,
        )

    def exchange(copy, here, total):
        for step in range(1, total):
            copy(lax.rem(here + step, total), here).start()
        for step in range(1, total):
            source = lax.rem(here + step, total)
            copy(source, source).wait_recv()

    def settle(copy, here, total):
        for step in range(1, total):
            copy(lax.rem(here + step, total), here).wait_send()

    near_land[mine] = param_ref[mine]
    exchange(near, mine, pairs)
    part = near_land[0]
    for slot in range(1, pairs):
        part = part + near_land[slot]
    far_land[place] = part
    exchange(far, place, count)
    part = far_land[0]
    for slot in range(1, count):
        part = part + far_land[slot]
    final_land[mine] = part
    exchange(final, mine, pairs)
    total_ref[...] = final_land[...]

    @pl.when(place == count - 1)
    def _():
        arrived_ref[...] = jnp.zeros_like(arrived_ref)

    @pl.when(place < count - 1)
    def _():
        back.wait_recv()
        arrived_ref[...] = back_land[...]

    settle(near, mine, pairs)
    settle(far, place, count)
    settle(final, mine, pairs)

    @pl.when(place > 0)
    def _():
        back.wait_send()


def final_kernel(
    q_ref, k_ref, v_ref, edge_ref, come_ref, total_ref, dq_ref, dk_ref, dv_ref, conv_ref, gain_ref, rate_ref
):
    length, width = q_ref.shape
    numbers, taps = conv_ref.shape[:2]
    heads = rate_ref.shape[1]
    size = width // heads
    for number, (ref, dst) in enumerate(((q_ref, dq_ref), (k_ref, dk_ref), (v_ref, dv_ref))):
        dst[...] = ref[...]
        part = slice(8 * number, 8 * number + 8)
        rows = edge_ref[part, :] + jnp.where(
            iota((8, width), 0) >= 9 - taps, come_ref[...].astype(F32)[part], 0.0
        )
        tile = jnp.concatenate([ref[length - TILE :, :].astype(F32)[0 : TILE - 8], rows], 0)
        dst[length - TILE :, :] = tile.astype(BF16)
    total = total_ref[...]
    for number in range(numbers):
        conv_ref[number] = total[number * taps : (number + 1) * taps]
    gain_ref[...] = total[12:13]
    rate = jnp.zeros(rate_ref.shape, F32)
    for head in range(heads):
        one = total[13:14, head * size : head * size + 1]
        rate = rate + jnp.where(iota(rate.shape, 1) == head, one, 0.0)
    rate_ref[...] = rate


def remote_params(number):
    return pltpu.CompilerParams(
        collective_id=number, has_side_effects=True, vmem_limit_bytes=VMEM_BYTES
    )


def body(
    q_raw,
    k_raw,
    v_raw,
    conv_weight,
    decay_logit,
    beta_logit,
    decay_rate,
    block_resets,
    norm_gain,
    d_out,
):
    tokens, width = q_raw.shape[1:]
    heads = decay_logit.shape[2]
    size = width // heads
    taps = conv_weight.shape[1]
    count = lax.axis_size("ctx")
    partners = lax.axis_size("head")
    pairs = lax.axis_size("dp")
    group = 4 if heads % 4 == 0 else 1
    steps = heads // group
    span = group * size
    vmem = pl.BlockSpec(memory_space=pltpu.VMEM)
    shape = jax.ShapeDtypeStruct
    dma = pltpu.SemaphoreType.DMA
    raws = (q_raw[0], k_raw[0], v_raw[0])
    gain = norm_gain[None, :]
    rate = decay_rate[None, :]
    decay, beta = decay_logit[0].T, beta_logit[0].T

    halo = pl.pallas_call(
        functools.partial(halo_kernel, count),
        out_shape=shape((3, TILE, width), BF16),
        in_specs=[pl.BlockSpec(memory_space=pl.ANY)] * 3,
        out_specs=vmem,
        scratch_shapes=[pltpu.VMEM((3, TILE, width), BF16), dma((3,)), dma((3,))],
        compiler_params=remote_params(0),
        name="halo",
    )(*raws)

    cols = pl.BlockSpec((tokens, span), lambda i: (0, i))
    halo_cols = pl.BlockSpec((3, TILE, span), lambda i: (0, 0, i))
    conv_cols = pl.BlockSpec((3, taps, span), lambda i: (0, 0, i))
    y_cols = pl.BlockSpec((3, tokens, span), lambda i: (0, 0, i))
    gate_all = pl.BlockSpec((heads, tokens), lambda i: (0, 0))
    rate_all = pl.BlockSpec((1, heads), lambda i: (0, 0))
    flag = pl.BlockSpec(memory_space=pltpu.SMEM)
    square = pl.BlockSpec((group, tokens, size), lambda i: (i, 0, 0))
    matrix = shape((heads, tokens, size), F32)
    local = pl.pallas_call(
        functools.partial(local_kernel, group),
        grid=(steps,),
        out_shape=[shape((3, tokens, width), F32)] + [matrix] * 10,
        in_specs=[cols] * 3 + [halo_cols, conv_cols, gate_all, gate_all, rate_all, flag],
        out_specs=[y_cols] + [square] * 10,
        scratch_shapes=[pltpu.VMEM((tokens + 8, span), F32)],
        compiler_params=pltpu.CompilerParams(vmem_limit_bytes=VMEM_BYTES),
        name="local",
    )(*raws, halo, conv_weight, decay, beta, rate, block_resets)
    y, query, key, inverse, attn, reach_key, base, reach, mix, carry_p, carry_q = local

    buffer = pltpu.VMEM((heads, size, size), F32)
    mixed, stat, state, grad = pl.pallas_call(
        functools.partial(chain_kernel, count, partners),
        out_shape=[
            shape((tokens, width), F32),
            shape((tokens, size), F32),
            shape((heads, size, size), F32),
            shape((heads, size, size), F32),
        ],
        in_specs=[vmem] * 6,
        out_specs=[vmem] * 4,
        scratch_shapes=[buffer] * 4
        + [pltpu.VMEM((partners, tokens, size), F32)]
        + [dma((heads,))] * 4
        + [dma((partners,))] * 2,
        compiler_params=remote_params(1),
        name="chain",
    )(mix, reach, carry_p, carry_q, d_out[0], gain)

    gain_cols = pl.BlockSpec((1, span), lambda i: (0, i))
    stat_all = pl.BlockSpec((tokens, size), lambda i: (0, 0))
    rows = lambda n: pl.BlockSpec((n, span), lambda i: (0, i))
    wide = shape((tokens, width), BF16)
    out, d_q, d_k, d_v, edge, back, param, d_decay, d_beta = pl.pallas_call(
        functools.partial(back_kernel, group, width * partners),
        grid=(steps,),
        out_shape=[wide] * 4
        + [
            shape((24, width), F32),
            shape((32, width), BF16),
            shape((16, width), F32),
            shape((heads, tokens), F32),
            shape((heads, tokens), F32),
        ],
        in_specs=[cols] * 3
        + [halo_cols, conv_cols, gate_all, gate_all, rate_all, flag]
        + [cols, gain_cols, cols, stat_all, y_cols]
        + [square] * 8,
        out_specs=[cols] * 4 + [rows(24), rows(32), rows(16), gate_all, gate_all],
        scratch_shapes=[
            pltpu.VMEM((tokens + 8, span), F32),
            pltpu.VMEM((tokens + 16, span), F32),
        ],
        compiler_params=pltpu.CompilerParams(vmem_limit_bytes=VMEM_BYTES),
        name="back",
    )(
        *raws, halo, conv_weight, decay, beta, rate, block_resets, d_out[0], gain, mixed, stat,
        y, query, key, inverse, attn, reach_key, base, state, grad,
    )

    rows_each = 16 // pairs
    total, arrived = pl.pallas_call(
        functools.partial(sum_kernel, count, pairs),
        out_shape=[shape((pairs, rows_each, width), F32), shape((32, width), BF16)],
        in_specs=[vmem] * 2,
        out_specs=[vmem] * 2,
        scratch_shapes=[
            pltpu.VMEM((pairs, rows_each, width), F32),
            pltpu.VMEM((count, rows_each, width), F32),
            pltpu.VMEM((pairs, rows_each, width), F32),
            pltpu.VMEM((32, width), BF16),
            dma((pairs,)),
            dma((pairs,)),
            dma((count,)),
            dma((count,)),
            dma((pairs,)),
            dma((pairs,)),
            dma,
            dma,
        ],
        compiler_params=remote_params(2),
        name="sums",
    )(param.reshape(pairs, rows_each, width), back)
    total = total.reshape(16, width)
    d_q, d_k, d_v, d_conv, d_gain, d_rate = pl.pallas_call(
        final_kernel,
        out_shape=[wide] * 3
        + [shape((3, taps, width), F32), shape((1, width), F32), shape((1, heads), F32)],
        in_specs=[vmem] * 6,
        out_specs=[vmem] * 6,
        compiler_params=pltpu.CompilerParams(vmem_limit_bytes=VMEM_BYTES),
        name="final",
    )(d_q, d_k, d_v, edge, arrived, total)
    return (
        out[None],
        d_q[None],
        d_k[None],
        d_v[None],
        d_conv,
        d_decay.T[None],
        d_beta.T[None],
        d_rate[0],
        d_gain[0],
    )


def solution(mesh):
    placed = (
        P("dp", "ctx", "head"),
        P("dp", "ctx", "head"),
        P("dp", "ctx", "head"),
        P(None, None, "head"),
        P("dp", "ctx", "head"),
        P("dp", "ctx", "head"),
        P("head"),
        P("dp", "ctx"),
        P("head"),
        P("dp", "ctx", "head"),
    )
    return jax.shard_map(
        body,
        mesh=mesh,
        in_specs=placed,
        out_specs=(
            P("dp", "ctx", "head"),
            P("dp", "ctx", "head"),
            P("dp", "ctx", "head"),
            P("dp", "ctx", "head"),
            P(None, None, "head"),
            P("dp", "ctx", "head"),
            P("dp", "ctx", "head"),
            P("head"),
            P("head"),
        ),
        check_vma=False,
    )
```

```python
import functools

import jax
import jax.numpy as jnp
from jax import lax
from jax.experimental import pallas as pl
from jax.experimental.pallas import tpu as pltpu
from jax.sharding import PartitionSpec as P

F32 = jnp.float32
BF16 = jnp.bfloat16
MESH = pl.DeviceIdType.MESH
VMEM_BYTES = 56 * 1024 * 1024
TILE = 16
EPS = 1e-06


def pair(x):
    hi = x.astype(BF16)
    return hi, (x - hi.astype(F32)).astype(BF16)


def dot_dims(a, b, dims):
    return lax.dot_general(a, b, (dims, ((), ())), preferred_element_type=F32)


def dot3(a, b, dims):
    return dot_dims(a[0], b[0], dims) + (dot_dims(a[0], b[1], dims) + dot_dims(a[1], b[0], dims))


NN = ((1,), (0,))
NT = ((1,), (1,))
TN = ((0,), (0,))


def iota(shape, dim):
    return lax.broadcasted_iota(jnp.int32, shape, dim)


def rows_sum(x):
    return jnp.sum(x, axis=1, keepdims=True)


def gates(logit, rate):
    soft = jnp.maximum(logit, 0.0) + jnp.log1p(jnp.exp(-jnp.abs(logit)))
    return soft, -rate * soft


def triple(x):
    hi, rest = pair(x)
    lo = (x - hi.astype(F32) - rest.astype(F32)).astype(BF16)
    return hi, rest, lo


def cumul_forms(gate):
    length = gate.shape[1]
    lower = (iota((length, length), 0) >= iota((length, length), 1)).astype(F32).astype(BF16)
    parts = triple(gate)
    col = sum(dot_dims(lower, p, NT) for p in parts)
    row = sum(dot_dims(p, lower, NT) for p in parts)
    return col, row


def pick_col(x, lane):
    return rows_sum(jnp.where(iota(x.shape, 1) == lane, x, 0.0))


def pick_row(x, sub):
    return jnp.sum(jnp.where(iota(x.shape, 0) == sub, x, 0.0), axis=0, keepdims=True)


def column(row):
    shape = (row.shape[1], row.shape[1])
    spot = iota(shape, 0) == iota(shape, 1)
    return rows_sum(jnp.where(spot, jnp.broadcast_to(row, shape), 0.0))


def greet(devices):
    barrier = pltpu.get_barrier_semaphore()
    for device in devices:
        pl.semaphore_signal(barrier, inc=1, device_id=device, device_id_type=MESH)
    pl.semaphore_wait(barrier, len(devices))


def ring_pair(count):
    place = lax.axis_index("ctx")
    return [{"ctx": lax.rem(place + 1, count)}, {"ctx": lax.rem(place + count - 1, count)}]


def others(axis, count):
    place = lax.axis_index(axis)
    return [{axis: lax.rem(place + step, count)} for step in range(1, count)]


def local_part(
    step,
    group,
    q_ref,
    k_ref,
    v_ref,
    halo_ref,
    conv_ref,
    decay_ref,
    beta_ref,
    rate_ref,
    reset_ref,
    y_ref,
    query_ref,
    key_ref,
    inv_ref,
    attn_ref,
    reach_key_ref,
    base_ref,
    reach_ref,
    mix_ref,
    carry_p_ref,
    carry_q_ref,
    padded,
):
    length, width = q_ref.shape
    size = width // group
    taps = conv_ref.shape[1]
    keep = (1 - reset_ref[0, 0]).astype(F32)
    acts = []
    for number, ref in enumerate((q_ref, k_ref, v_ref)):
        padded[0:8, :] = halo_ref[number].astype(F32)[TILE - 8 :] * keep
        padded[8 : 8 + length, :] = ref[...].astype(F32)
        total = conv_ref[number, 0:1, :] * padded[8 : 8 + length, :]
        for tap in range(1, taps):
            total = total + conv_ref[number, tap : tap + 1, :] * padded[8 - tap : 8 - tap + length, :]
        y_ref[number] = total
        acts.append(total * jax.nn.sigmoid(total))
    gate = gates(decay_ref[...], column(rate_ref[...]))[1]
    cumul_col, cumul_row = cumul_forms(gate)
    write_all = jax.nn.sigmoid(beta_ref[...])
    row_i = iota((length, length), 0)
    col_i = iota((length, length), 1)
    eye = (row_i == col_i).astype(F32)
    heads = range(group)
    state = []
    for j in heads:
        head = step * group + j
        cols = slice(j * size, (j + 1) * size)
        act_q, act_k, value = acts[0][:, cols], acts[1][:, cols], acts[2][:, cols]
        query = act_q * lax.rsqrt(rows_sum(act_q * act_q) + EPS) * size ** (-0.5)
        key = act_k * lax.rsqrt(rows_sum(act_k * act_k) + EPS)
        query_ref[j] = query
        key_ref[j] = key
        col = pick_col(cumul_col, head)
        row = pick_row(cumul_row, head)
        write = column(pick_row(write_all, head))
        spread = jnp.exp(jnp.minimum(col - row, 0.0))
        key_pair = pair(key)
        query_pair = pair(query)
        inner = dot3(key_pair, pair(write * key), NT)
        system = jnp.where(row_i > col_i, spread * inner, 0.0)
        attn = jnp.where(row_i >= col_i, spread * dot3(query_pair, key_pair, NT), 0.0)
        attn_ref[j] = attn
        state.append((key, query, value, col, write, system, attn, key_pair))
    inverse = [
        eye - jnp.where((row_i >> 1) == (col_i >> 1), state[j][5], 0.0) for j in heads
    ]
    level = 1
    while (2 << level) <= length:
        mask = ((row_i >> (level + 1)) == (col_i >> (level + 1))) & (
            (row_i >> level) != (col_i >> level)
        )
        pairs = [pair(inverse[j]) for j in heads]
        middle = [
            dot3(pairs[j], pair(jnp.where(mask, state[j][5], 0.0)), NN) for j in heads
        ]
        inverse = [inverse[j] - dot3(pair(middle[j]), pairs[j], NN) for j in heads]
        level += 1
    for j in heads:
        key, query, value, col, write, system, attn, key_pair = state[j]
        inv_ref[j] = inverse[j]
        inv_pair = pair(inverse[j])
        growth = jnp.exp(col)
        last = col[length - 1 : length, :]
        tail = jnp.exp(last - col)
        base = dot3(inv_pair, pair(value), NN)
        reach_key = dot3(inv_pair, pair(growth * key), NN)
        base_ref[j] = base
        reach_key_ref[j] = reach_key
        attn_pair = pair(attn)
        wide_base = write * base
        wide_reach = write * reach_key
        mix_ref[j] = dot3(attn_pair, pair(wide_base), NN)
        reach_ref[j] = keep * (growth * query - dot3(attn_pair, pair(wide_reach), NN))
        carry_q_ref[j] = dot3(pair(tail * wide_base), key_pair, TN)
        carry_p_ref[j] = keep * (
            jnp.exp(last) * eye - dot3(pair(tail * wide_reach), key_pair, TN)
        )


def back_part(
    step,
    group,
    full_width,
    q_ref,
    k_ref,
    v_ref,
    halo_ref,
    conv_ref,
    decay_ref,
    beta_ref,
    rate_ref,
    reset_ref,
    d_out_ref,
    gain_ref,
    mixed_ref,
    stat_ref,
    y_ref,
    query_ref,
    key_ref,
    inv_ref,
    attn_ref,
    reach_key_ref,
    base_ref,
    state_ref,
    grad_ref,
    out_ref,
    dq_ref,
    dk_ref,
    dv_ref,
    edge_ref,
    back_ref,
    param_ref,
    d_decay_ref,
    d_beta_ref,
    padded,
    d_conv,
):
    length, width = q_ref.shape
    size = width // group
    taps = conv_ref.shape[1]
    keep = (1 - reset_ref[0, 0]).astype(F32)
    stat = stat_ref[...]
    scale = lax.rsqrt(stat[:, 0:1] / full_width + EPS)
    coef = scale * scale * scale * stat[:, size - 1 : size] / full_width
    mixed = mixed_ref[...]
    grad_y = d_out_ref[...].astype(F32)
    gain = gain_ref[...]
    normal = mixed * scale
    out_ref[...] = (normal * gain).astype(BF16)
    param_ref[...] = jnp.zeros_like(param_ref)
    param_ref[12:13, :] = jnp.sum(grad_y * normal, axis=0, keepdims=True)
    grad_mixed = grad_y * gain * scale - mixed * coef

    rate = column(rate_ref[...])
    soft, gate = gates(decay_ref[...], rate)
    slope = jax.nn.sigmoid(decay_ref[...])
    cumul_col, cumul_row = cumul_forms(gate)
    write_all = jax.nn.sigmoid(beta_ref[...])
    row_i = iota((length, length), 0)
    col_i = iota((length, length), 1)
    upper = (row_i <= col_i).astype(F32).astype(BF16)
    gathered = jnp.zeros((length, size), F32)
    half = size // 2

    @pl.when(step == 0)
    def _():
        d_decay_ref[...] = jnp.zeros_like(d_decay_ref)
        d_beta_ref[...] = jnp.zeros_like(d_beta_ref)

    heads = range(group)
    pre = []
    for j in heads:
        cols = slice(j * size, (j + 1) * size)
        head = step * group + j
        col = pick_col(cumul_col, head)
        row = pick_row(cumul_row, head)
        write = column(pick_row(write_all, head))
        spread = jnp.exp(jnp.minimum(col - row, 0.0))
        growth = jnp.exp(col)
        last = col[length - 1 : length, :]
        tail = jnp.exp(last - col)
        query, key = query_ref[j], key_ref[j]
        entering = keep * state_ref[j]
        leaving = grad_ref[j]
        enter_pair, leave_pair = pair(entering), pair(leaving)
        key_pair, query_pair = pair(key), pair(query)
        grad = grad_mixed[:, cols]
        grad_pair = pair(grad)
        delta = base_ref[j] - dot3(pair(reach_key_ref[j]), enter_pair, NT)
        used = write * delta
        used_pair = pair(used)
        d_used = dot3(pair(attn_ref[j]), grad_pair, TN) + tail * dot3(key_pair, leave_pair, NT)
        d_attn = jnp.where(row_i >= col_i, spread * dot3(grad_pair, used_pair, NT), 0.0)
        d_attn_pair = pair(d_attn)
        d_query = growth * dot3(grad_pair, enter_pair, NN) + dot3(d_attn_pair, key_pair, NN)
        d_key_tail = tail * dot3(used_pair, leave_pair, NN)
        d_key_plus = dot3(d_attn_pair, query_pair, TN) + d_key_tail
        right = dot3(pair(inv_ref[j]), pair(write * d_used), TN)
        right_pair = pair(right)
        d_system = jnp.where(row_i > col_i, -spread * dot3(right_pair, pair(delta), NT), 0.0)
        d_system_pair = pair(d_system)
        d_inner = dot3(d_system_pair, key_pair, TN)
        d_key_minus = dot3(d_system_pair, pair(write * key), NN) - growth * dot3(
            right_pair, enter_pair, NN
        )
        d_key_plus = d_key_plus + write * d_inner
        d_write = rows_sum(d_used * delta + key * d_inner)
        whole = jnp.sum(rows_sum(key * d_key_tail), axis=0, keepdims=True) + jnp.exp(
            last
        ) * jnp.sum(rows_sum(leaving * entering), axis=0, keepdims=True)
        d_cumul = rows_sum(query * d_query + key * (d_key_minus - d_key_plus))
        spot = jnp.where(iota(d_cumul.shape, 0) == length - 1, whole, 0.0)
        d_key = d_key_plus + d_key_minus
        gathered = gathered + jnp.where(col_i == head, d_cumul + spot, 0.0)
        gathered = gathered + jnp.where(col_i == half + head, d_write, 0.0)
        pre.append((d_query, d_key, right))

    turned = gathered.T
    count = decay_ref.shape[0]
    d_gate = sum(dot_dims(p, upper, NT) for p in pair(turned[0:count]))
    d_decay_ref[...] += -rate * slope * d_gate
    d_beta_ref[...] += turned[half : half + count] * write_all * (1.0 - write_all)
    d_rate = -rows_sum(soft * d_gate)
    for j in heads:
        one = pick_row(d_rate, step * group + j)
        param_ref[13:14, j * size : (j + 1) * size] = jnp.broadcast_to(one, (1, size))

    rooted = size ** (-0.5)
    back_ref[...] = jnp.zeros_like(back_ref)
    for number, (ref, dst) in enumerate(((q_ref, dq_ref), (k_ref, dk_ref), (v_ref, dv_ref))):
        d_conv[0:8, :] = jnp.zeros((8, width), F32)
        d_conv[8 + length :, :] = jnp.zeros((8, width), F32)
        padded[0:8, :] = halo_ref[number].astype(F32)[TILE - 8 :] * keep
        padded[8 : 8 + length, :] = ref[...].astype(F32)
        for j in heads:
            cols = slice(j * size, (j + 1) * size)
            total = y_ref[number, :, cols]
            gated = jax.nn.sigmoid(total)
            grad = pre[j][number]
            if number < 2:
                act = total * gated
                inv_norm = lax.rsqrt(rows_sum(act * act) + EPS)
                unit = act * inv_norm
                if number == 0:
                    grad = grad * rooted
                grad = inv_norm * (grad - unit * rows_sum(unit * grad))
            d_conv[8 : 8 + length, cols] = grad * (gated * (1.0 + total * (1.0 - gated)))
        grad = d_conv[8 : 8 + length, :]
        extended = conv_ref[number, 0:1, :] * d_conv[0 : 8 + length, :]
        param_ref[4 * number : 4 * number + 1, :] = jnp.sum(
            grad * padded[8 : 8 + length, :], axis=0, keepdims=True
        )
        for tap in range(1, taps):
            extended = extended + conv_ref[number, tap : tap + 1, :] * d_conv[tap : tap + 8 + length, :]
            param_ref[4 * number + tap : 4 * number + tap + 1, :] = jnp.sum(
                grad * padded[8 - tap : 8 - tap + length, :], axis=0, keepdims=True
            )
        dst[...] = extended[8:].astype(BF16)
        edge_ref[8 * number : 8 * number + 8, :] = extended[length:]
        back_ref[8 * number : 8 * number + 8, :] = (keep * extended[0:8]).astype(BF16)


def mixer_kernel(
    count,
    partners,
    pairs,
    group,
    q_ref,
    k_ref,
    v_ref,
    conv_ref,
    decay_ref,
    beta_ref,
    rate_ref,
    reset_ref,
    d_out_ref,
    gain_ref,
    out_ref,
    dq_ref,
    dk_ref,
    dv_ref,
    edge_ref,
    d_decay_ref,
    d_beta_ref,
    total_ref,
    arrived_ref,
    y_ref,
    query_ref,
    key_ref,
    inv_ref,
    attn_ref,
    reach_key_ref,
    base_ref,
    reach_ref,
    mix_ref,
    carry_p_ref,
    carry_q_ref,
    state_ref,
    grad_ref,
    state_land,
    state_out,
    grad_land,
    grad_out,
    mixed_ref,
    stat_ref,
    stat_land,
    halo_ref,
    halo_land,
    back_ref,
    back_land,
    param_ref,
    near_land,
    far_land,
    final_land,
    padded,
    d_conv,
    halo_send,
    halo_recv,
    state_send,
    state_recv,
    grad_send,
    grad_recv,
    stat_send,
    stat_recv,
    near_send,
    near_recv,
    far_send,
    far_recv,
    final_send,
    final_recv,
    back_send,
    back_recv,
):
    place = lax.axis_index("ctx")
    core = lax.axis_index("dp")
    heads, length, size = mix_ref.shape
    steps = heads // group
    span = group * size
    rows = param_ref.shape[0] // pairs
    full_width = heads * size * partners
    raws = (q_ref, k_ref, v_ref)
    kept = (query_ref, key_ref, inv_ref, attn_ref, reach_key_ref, base_ref)
    greet(others("ctx", count) + others("head", partners) + others("dp", pairs))

    def halo_copy(number):
        return pltpu.make_async_remote_copy(
            src_ref=raws[number].at[pl.ds(length - TILE, TILE)],
            dst_ref=halo_land.at[number],
            send_sem=halo_send.at[number],
            recv_sem=halo_recv.at[number],
            device_id={"ctx": lax.rem(place + 1, count)},
            device_id_type=MESH,
        )

    @pl.when(place < count - 1)
    def _():
        for number in range(3):
            halo_copy(number).start()

    @pl.when(place == 0)
    def _():
        halo_ref[...] = jnp.zeros_like(halo_ref)

    @pl.when(place > 0)
    def _():
        for number in range(3):
            halo_copy(number).wait_recv()
        halo_ref[...] = halo_land[...]

    @pl.when(place < count - 1)
    def _():
        for number in range(3):
            halo_copy(number).wait_send()

    def state_copy(h):
        return pltpu.make_async_remote_copy(
            src_ref=state_out.at[h],
            dst_ref=state_land.at[h],
            send_sem=state_send.at[h],
            recv_sem=state_recv.at[h],
            device_id={"ctx": lax.rem(place + 1, count)},
            device_id_type=MESH,
        )

    def grad_copy(h):
        return pltpu.make_async_remote_copy(
            src_ref=grad_out.at[h],
            dst_ref=grad_land.at[h],
            send_sem=grad_send.at[h],
            recv_sem=grad_recv.at[h],
            device_id={"ctx": lax.rem(place + count - 1, count)},
            device_id_type=MESH,
        )

    def forward(step, carry):
        wide = pl.ds(pl.multiple_of(step * span, span), span)
        some = pl.ds(step * group, group)
        local_part(
            step,
            group,
            *[ref.at[:, wide] for ref in raws],
            halo_ref.at[:, :, wide],
            conv_ref.at[:, :, wide],
            decay_ref,
            beta_ref,
            rate_ref,
            reset_ref,
            y_ref.at[:, :, wide],
            *[ref.at[some] for ref in (*kept, reach_ref, mix_ref, carry_p_ref, carry_q_ref)],
            padded,
        )

        @pl.when(place == 0)
        def _():
            for j in range(group):
                h = step * group + j
                state_ref[h] = jnp.zeros((size, size), F32)
                state_out[h] = carry_q_ref[h]
                if count > 1:
                    state_copy(h).start()

        return carry

    lax.fori_loop(0, steps, forward, 0)

    @pl.when(place > 0)
    def _():
        def hop(h, carry):
            state_copy(h).wait_recv()
            entering = state_land[h]
            state_ref[h] = entering

            @pl.when(place < count - 1)
            def _():
                state_out[h] = carry_q_ref[h] + dot3(pair(entering), pair(carry_p_ref[h]), NN)
                state_copy(h).start()

            return carry

        lax.fori_loop(0, heads, hop, 0)

    def mixing(h, carry):
        square, inner = carry
        cols = pl.ds(pl.multiple_of(h * size, size), size)
        mixed = mix_ref[h] + dot3(pair(reach_ref[h]), pair(state_ref[h]), NT)
        mixed_ref[:, cols] = mixed
        weighted = d_out_ref[:, cols].astype(F32) * gain_ref[:, cols]
        return square + mixed * mixed, inner + weighted * mixed

    zero = jnp.zeros((length, size), F32)
    square, inner = lax.fori_loop(0, heads, mixing, (zero, zero))
    half = iota((length, size), 1) < size // 2
    mine = lax.axis_index("head")
    stat_land[mine] = jnp.where(half, rows_sum(square), rows_sum(inner))

    def stat_copy(target, slot):
        return pltpu.make_async_remote_copy(
            src_ref=stat_land.at[mine],
            dst_ref=stat_land.at[slot],
            send_sem=stat_send.at[target],
            recv_sem=stat_recv.at[slot],
            device_id={"head": target},
            device_id_type=MESH,
        )

    for step in range(1, partners):
        stat_copy(lax.rem(mine + step, partners), mine).start()
    for step in range(1, partners):
        source = lax.rem(mine + step, partners)
        stat_copy(source, source).wait_recv()
    stat = stat_land[0]
    for slot in range(1, partners):
        stat = stat + stat_land[slot]
    stat_ref[...] = stat
    scale = lax.rsqrt(stat[:, 0:1] / full_width + EPS)
    coef = scale * scale * scale * stat[:, size - 1 : size] / full_width

    def source_grad(h, carry):
        cols = pl.ds(pl.multiple_of(h * size, size), size)
        weighted = d_out_ref[:, cols].astype(F32) * gain_ref[:, cols]
        grad_mixed = weighted * scale - mixed_ref[:, cols] * coef
        grad_out[h] = dot3(pair(grad_mixed), pair(reach_ref[h]), TN)

        @pl.when((place == count - 1) & (place > 0))
        def _():
            grad_copy(h).start()

        return carry

    @pl.when(place > 0)
    def _():
        lax.fori_loop(0, heads, source_grad, 0)

    @pl.when(place == count - 1)
    def _():
        grad_ref[...] = jnp.zeros_like(grad_ref)

    def hop(h, carry):
        grad_copy(h).wait_recv()
        leaving = grad_land[h]
        grad_ref[h] = leaving

        @pl.when(place > 0)
        def _():
            grad_out[h] = grad_out[h] + dot3(pair(leaving), pair(carry_p_ref[h]), NT)
            grad_copy(h).start()

        return carry

    def backward(step, carry):
        wide = pl.ds(pl.multiple_of(step * span, span), span)
        some = pl.ds(step * group, group)

        @pl.when((place < count - 1) & (place > 0) & (step == 0))
        def _():
            lax.fori_loop(0, heads, hop, 0)

        @pl.when((place < count - 1) & (place == 0))
        def _():
            lax.fori_loop(step * group, step * group + group, hop, 0)

        back_part(
            step,
            group,
            full_width,
            *[ref.at[:, wide] for ref in raws],
            halo_ref.at[:, :, wide],
            conv_ref.at[:, :, wide],
            decay_ref,
            beta_ref,
            rate_ref,
            reset_ref,
            d_out_ref.at[:, wide],
            gain_ref.at[:, wide],
            mixed_ref.at[:, wide],
            stat_ref,
            y_ref.at[:, :, wide],
            *[ref.at[some] for ref in (*kept, state_ref, grad_ref)],
            *[ref.at[:, wide] for ref in (out_ref, dq_ref, dk_ref, dv_ref, edge_ref, back_ref, param_ref)],
            d_decay_ref,
            d_beta_ref,
            padded,
            d_conv,
        )
        return carry

    lax.fori_loop(0, steps, backward, 0)

    for step in range(1, partners):
        stat_copy(lax.rem(mine + step, partners), mine).wait_send()

    @pl.when(place < count - 1)
    def _():
        def done(h, carry):
            state_copy(h).wait_send()
            return carry

        lax.fori_loop(0, heads, done, 0)

    @pl.when(place > 0)
    def _():
        def done(h, carry):
            grad_copy(h).wait_send()
            return carry

        lax.fori_loop(0, heads, done, 0)

    back = pltpu.make_async_remote_copy(
        src_ref=back_ref,
        dst_ref=back_land,
        send_sem=back_send,
        recv_sem=back_recv,
        device_id={"ctx": lax.rem(place + count - 1, count)},
        device_id_type=MESH,
    )

    @pl.when(place > 0)
    def _():
        back.start()

    def near(target, slot):
        return pltpu.make_async_remote_copy(
            src_ref=param_ref.at[pl.ds(pl.multiple_of(target * rows, rows), rows)],
            dst_ref=near_land.at[slot],
            send_sem=near_send.at[target],
            recv_sem=near_recv.at[slot],
            device_id={"dp": target},
            device_id_type=MESH,
        )

    def far(target, slot):
        return pltpu.make_async_remote_copy(
            src_ref=far_land.at[place],
            dst_ref=far_land.at[slot],
            send_sem=far_send.at[target],
            recv_sem=far_recv.at[slot],
            device_id={"ctx": target},
            device_id_type=MESH,
        )

    def final(target, slot):
        return pltpu.make_async_remote_copy(
            src_ref=final_land.at[core],
            dst_ref=final_land.at[slot],
            send_sem=final_send.at[target],
            recv_sem=final_recv.at[slot],
            device_id={"dp": target},
            device_id_type=MESH,
        )

    def exchange(copy, here, total):
        for step in range(1, total):
            copy(lax.rem(here + step, total), here).start()
        for step in range(1, total):
            source = lax.rem(here + step, total)
            copy(source, source).wait_recv()

    def settle(copy, here, total):
        for step in range(1, total):
            copy(lax.rem(here + step, total), here).wait_send()

    near_land[core] = param_ref[pl.ds(pl.multiple_of(core * rows, rows), rows), :]
    exchange(near, core, pairs)
    part = near_land[0]
    for slot in range(1, pairs):
        part = part + near_land[slot]
    far_land[place] = part
    exchange(far, place, count)
    part = far_land[0]
    for slot in range(1, count):
        part = part + far_land[slot]
    final_land[core] = part
    exchange(final, core, pairs)
    total_ref[...] = final_land[...]

    @pl.when(place == count - 1)
    def _():
        arrived_ref[...] = jnp.zeros_like(arrived_ref)

    @pl.when(place < count - 1)
    def _():
        back.wait_recv()
        arrived_ref[...] = back_land[...]

    settle(near, core, pairs)
    settle(far, place, count)
    settle(final, core, pairs)

    @pl.when(place > 0)
    def _():
        back.wait_send()


def final_kernel(
    o_ref, decay_ref, beta_ref, q_ref, k_ref, v_ref, edge_ref, come_ref, total_ref,
    out_ref, d_decay_ref, d_beta_ref, dq_ref, dk_ref, dv_ref, conv_ref, gain_ref, rate_ref,
):
    out_ref[...] = o_ref[...]
    d_decay_ref[...] = decay_ref[...]
    d_beta_ref[...] = beta_ref[...]
    length, width = q_ref.shape
    numbers, taps = conv_ref.shape[:2]
    heads = rate_ref.shape[1]
    size = width // heads
    for number, (ref, dst) in enumerate(((q_ref, dq_ref), (k_ref, dk_ref), (v_ref, dv_ref))):
        dst[...] = ref[...]
        part = slice(8 * number, 8 * number + 8)
        rows = edge_ref[part, :] + jnp.where(
            iota((8, width), 0) >= 9 - taps, come_ref[...].astype(F32)[part], 0.0
        )
        tile = jnp.concatenate([ref[length - TILE :, :].astype(F32)[0 : TILE - 8], rows], 0)
        dst[length - TILE :, :] = tile.astype(BF16)
    total = total_ref[...]
    for number in range(numbers):
        conv_ref[number] = total[number * taps : (number + 1) * taps]
    gain_ref[...] = total[12:13]
    rate = jnp.zeros(rate_ref.shape, F32)
    for head in range(heads):
        one = total[13:14, head * size : head * size + 1]
        rate = rate + jnp.where(iota(rate.shape, 1) == head, one, 0.0)
    rate_ref[...] = rate


def remote_params(number):
    return pltpu.CompilerParams(
        collective_id=number, has_side_effects=True, vmem_limit_bytes=VMEM_BYTES
    )


def body(
    q_raw,
    k_raw,
    v_raw,
    conv_weight,
    decay_logit,
    beta_logit,
    decay_rate,
    block_resets,
    norm_gain,
    d_out,
):
    tokens, width = q_raw.shape[1:]
    heads = decay_logit.shape[2]
    size = width // heads
    taps = conv_weight.shape[1]
    count = lax.axis_size("ctx")
    partners = lax.axis_size("head")
    pairs = lax.axis_size("dp")
    group = 4 if heads % 4 == 0 else 1
    span = group * size
    vmem = pl.BlockSpec(memory_space=pltpu.VMEM)
    shape = jax.ShapeDtypeStruct
    dma = pltpu.SemaphoreType.DMA
    raws = (q_raw[0], k_raw[0], v_raw[0])
    gain = norm_gain[None, :]
    rate = decay_rate[None, :]
    decay, beta = decay_logit[0].T, beta_logit[0].T

    flag = pl.BlockSpec(memory_space=pltpu.SMEM)
    wide = shape((tokens, width), BF16)
    gate = shape((heads, tokens), F32)
    lines = 16
    part = lines // pairs
    buffer = pltpu.VMEM((heads, tokens, size), F32)
    square = pltpu.VMEM((heads, size, size), F32)
    out, d_q, d_k, d_v, edge, d_decay, d_beta, total, arrived = pl.pallas_call(
        functools.partial(mixer_kernel, count, partners, pairs, group),
        out_shape=[wide] * 4
        + [
            shape((24, width), F32),
            gate,
            gate,
            shape((pairs, part, width), F32),
            shape((32, width), BF16),
        ],
        in_specs=[vmem] * 7 + [flag] + [vmem] * 2,
        out_specs=[vmem] * 9,
        scratch_shapes=[pltpu.VMEM((3, tokens, width), F32)]
        + [buffer] * 8
        + [square] * 8
        + [
            pltpu.VMEM((tokens, width), F32),
            pltpu.VMEM((tokens, size), F32),
            pltpu.VMEM((partners, tokens, size), F32),
            pltpu.VMEM((3, TILE, width), BF16),
            pltpu.VMEM((3, TILE, width), BF16),
            pltpu.VMEM((32, width), BF16),
            pltpu.VMEM((32, width), BF16),
            pltpu.VMEM((lines, width), F32),
            pltpu.VMEM((pairs, part, width), F32),
            pltpu.VMEM((count, part, width), F32),
            pltpu.VMEM((pairs, part, width), F32),
            pltpu.VMEM((tokens + 8, span), F32),
            pltpu.VMEM((tokens + 16, span), F32),
        ]
        + [dma((3,))] * 2
        + [dma((heads,))] * 4
        + [dma((partners,))] * 2
        + [dma((pairs,))] * 2
        + [dma((count,))] * 2
        + [dma((pairs,))] * 2
        + [dma] * 2,
        compiler_params=remote_params(0),
        name="mixer",
    )(*raws, conv_weight, decay, beta, rate, block_resets, d_out[0], gain)
    total = total.reshape(16, width)
    out, d_decay, d_beta, d_q, d_k, d_v, d_conv, d_gain, d_rate = pl.pallas_call(
        final_kernel,
        out_shape=[wide, gate, gate]
        + [wide] * 3
        + [shape((3, taps, width), F32), shape((1, width), F32), shape((1, heads), F32)],
        in_specs=[vmem] * 9,
        out_specs=[vmem] * 9,
        compiler_params=pltpu.CompilerParams(vmem_limit_bytes=VMEM_BYTES),
        name="final",
    )(out, d_decay, d_beta, d_q, d_k, d_v, edge, arrived, total)
    return (
        out[None],
        d_q[None],
        d_k[None],
        d_v[None],
        d_conv,
        d_decay.T[None],
        d_beta.T[None],
        d_rate[0],
        d_gain[0],
    )


def solution(mesh):
    placed = (
        P("dp", "ctx", "head"),
        P("dp", "ctx", "head"),
        P("dp", "ctx", "head"),
        P(None, None, "head"),
        P("dp", "ctx", "head"),
        P("dp", "ctx", "head"),
        P("head"),
        P("dp", "ctx"),
        P("head"),
        P("dp", "ctx", "head"),
    )
    return jax.shard_map(
        body,
        mesh=mesh,
        in_specs=placed,
        out_specs=(
            P("dp", "ctx", "head"),
            P("dp", "ctx", "head"),
            P("dp", "ctx", "head"),
            P("dp", "ctx", "head"),
            P(None, None, "head"),
            P("dp", "ctx", "head"),
            P("dp", "ctx", "head"),
            P("head"),
            P("head"),
        ),
        check_vma=False,
    )
```

```python
import functools

import jax
import jax.numpy as jnp
from jax import lax
from jax.experimental import pallas as pl
from jax.experimental.pallas import tpu as pltpu
from jax.sharding import PartitionSpec as P

F32 = jnp.float32
BF16 = jnp.bfloat16
MESH = pl.DeviceIdType.MESH
VMEM_BYTES = 56 * 1024 * 1024
TILE = 16
EPS = 1e-06


def pair(x):
    hi = x.astype(BF16)
    return hi, (x - hi.astype(F32)).astype(BF16)


def dot_dims(a, b, dims):
    return lax.dot_general(a, b, (dims, ((), ())), preferred_element_type=F32)


def dot3(a, b, dims):
    return dot_dims(a[0], b[0], dims) + (dot_dims(a[0], b[1], dims) + dot_dims(a[1], b[0], dims))


NN = ((1,), (0,))
NT = ((1,), (1,))
TN = ((0,), (0,))


def iota(shape, dim):
    return lax.broadcasted_iota(jnp.int32, shape, dim)


def rows_sum(x):
    return jnp.sum(x, axis=1, keepdims=True)


def gates(logit, rate):
    soft = jnp.maximum(logit, 0.0) + jnp.log1p(jnp.exp(-jnp.abs(logit)))
    return soft, -rate * soft


def triple(x):
    hi, rest = pair(x)
    lo = (x - hi.astype(F32) - rest.astype(F32)).astype(BF16)
    return hi, rest, lo


def cumul_forms(gate):
    length = gate.shape[1]
    lower = (iota((length, length), 0) >= iota((length, length), 1)).astype(F32).astype(BF16)
    parts = triple(gate)
    col = sum(dot_dims(lower, p, NT) for p in parts)
    row = sum(dot_dims(p, lower, NT) for p in parts)
    return col, row


def pick_col(x, lane):
    return rows_sum(jnp.where(iota(x.shape, 1) == lane, x, 0.0))


def pick_row(x, sub):
    return jnp.sum(jnp.where(iota(x.shape, 0) == sub, x, 0.0), axis=0, keepdims=True)


def column(row):
    shape = (row.shape[1], row.shape[1])
    spot = iota(shape, 0) == iota(shape, 1)
    return rows_sum(jnp.where(spot, jnp.broadcast_to(row, shape), 0.0))


def greet(devices):
    barrier = pltpu.get_barrier_semaphore()
    for device in devices:
        pl.semaphore_signal(barrier, inc=1, device_id=device, device_id_type=MESH)
    pl.semaphore_wait(barrier, len(devices))


def ring_pair(count):
    place = lax.axis_index("ctx")
    return [{"ctx": lax.rem(place + 1, count)}, {"ctx": lax.rem(place + count - 1, count)}]


def others(axis, count):
    place = lax.axis_index(axis)
    return [{axis: lax.rem(place + step, count)} for step in range(1, count)]


def local_part(
    step,
    group,
    q_ref,
    k_ref,
    v_ref,
    halo_ref,
    conv_ref,
    decay_ref,
    beta_ref,
    rate_ref,
    reset_ref,
    y_ref,
    query_ref,
    key_ref,
    inv_ref,
    attn_ref,
    reach_key_ref,
    base_ref,
    reach_ref,
    mix_ref,
    carry_p_ref,
    carry_q_ref,
    padded,
):
    length, width = q_ref.shape
    size = width // group
    taps = conv_ref.shape[1]
    keep = (1 - reset_ref[0, 0]).astype(F32)
    acts = []
    for number, ref in enumerate((q_ref, k_ref, v_ref)):
        padded[0:8, :] = halo_ref[number].astype(F32)[TILE - 8 :] * keep
        padded[8 : 8 + length, :] = ref[...].astype(F32)
        total = conv_ref[number, 0:1, :] * padded[8 : 8 + length, :]
        for tap in range(1, taps):
            total = total + conv_ref[number, tap : tap + 1, :] * padded[8 - tap : 8 - tap + length, :]
        y_ref[number] = total
        acts.append(total * jax.nn.sigmoid(total))
    gate = gates(decay_ref[...], column(rate_ref[...]))[1]
    cumul_col, cumul_row = cumul_forms(gate)
    write_all = jax.nn.sigmoid(beta_ref[...])
    row_i = iota((length, length), 0)
    col_i = iota((length, length), 1)
    eye = (row_i == col_i).astype(F32)
    heads = range(group)
    state = []
    for j in heads:
        head = step * group + j
        cols = slice(j * size, (j + 1) * size)
        act_q, act_k, value = acts[0][:, cols], acts[1][:, cols], acts[2][:, cols]
        query = act_q * lax.rsqrt(rows_sum(act_q * act_q) + EPS) * size ** (-0.5)
        key = act_k * lax.rsqrt(rows_sum(act_k * act_k) + EPS)
        query_ref[j] = query
        key_ref[j] = key
        col = pick_col(cumul_col, head)
        row = pick_row(cumul_row, head)
        write = column(pick_row(write_all, head))
        spread = jnp.exp(jnp.minimum(col - row, 0.0))
        key_pair = pair(key)
        query_pair = pair(query)
        inner = dot3(key_pair, pair(write * key), NT)
        system = jnp.where(row_i > col_i, spread * inner, 0.0)
        attn = jnp.where(row_i >= col_i, spread * dot3(query_pair, key_pair, NT), 0.0)
        attn_ref[j] = attn
        state.append((key, query, value, col, write, system, attn, key_pair))
    inverse = [
        eye - jnp.where((row_i >> 1) == (col_i >> 1), state[j][5], 0.0) for j in heads
    ]
    level = 1
    while (2 << level) <= length:
        mask = ((row_i >> (level + 1)) == (col_i >> (level + 1))) & (
            (row_i >> level) != (col_i >> level)
        )
        pairs = [pair(inverse[j]) for j in heads]
        middle = [
            dot3(pairs[j], pair(jnp.where(mask, state[j][5], 0.0)), NN) for j in heads
        ]
        inverse = [inverse[j] - dot3(pair(middle[j]), pairs[j], NN) for j in heads]
        level += 1
    for j in heads:
        key, query, value, col, write, system, attn, key_pair = state[j]
        inv_ref[j] = inverse[j]
        inv_pair = pair(inverse[j])
        growth = jnp.exp(col)
        last = col[length - 1 : length, :]
        tail = jnp.exp(last - col)
        base = dot3(inv_pair, pair(value), NN)
        reach_key = dot3(inv_pair, pair(growth * key), NN)
        base_ref[j] = base
        reach_key_ref[j] = reach_key
        attn_pair = pair(attn)
        wide_base = write * base
        wide_reach = write * reach_key
        mix_ref[j] = dot3(attn_pair, pair(wide_base), NN)
        reach_ref[j] = keep * (growth * query - dot3(attn_pair, pair(wide_reach), NN))
        carry_q_ref[j] = dot3(pair(tail * wide_base), key_pair, TN)
        carry_p_ref[j] = keep * (
            jnp.exp(last) * eye - dot3(pair(tail * wide_reach), key_pair, TN)
        )


def back_part(
    step,
    group,
    full_width,
    q_ref,
    k_ref,
    v_ref,
    halo_ref,
    conv_ref,
    decay_ref,
    beta_ref,
    rate_ref,
    reset_ref,
    d_out_ref,
    gain_ref,
    mixed_ref,
    stat_ref,
    y_ref,
    query_ref,
    key_ref,
    inv_ref,
    attn_ref,
    reach_key_ref,
    base_ref,
    state_ref,
    grad_ref,
    out_ref,
    dq_ref,
    dk_ref,
    dv_ref,
    edge_ref,
    back_ref,
    param_ref,
    d_decay_ref,
    d_beta_ref,
    padded,
    d_conv,
):
    length, width = q_ref.shape
    size = width // group
    taps = conv_ref.shape[1]
    keep = (1 - reset_ref[0, 0]).astype(F32)
    stat = stat_ref[...]
    scale = lax.rsqrt(stat[:, 0:1] / full_width + EPS)
    coef = scale * scale * scale * stat[:, size - 1 : size] / full_width
    mixed = mixed_ref[...]
    grad_y = d_out_ref[...].astype(F32)
    gain = gain_ref[...]
    normal = mixed * scale
    out_ref[...] = (normal * gain).astype(BF16)
    param_ref[...] = jnp.zeros_like(param_ref)
    param_ref[12:13, :] = jnp.sum(grad_y * normal, axis=0, keepdims=True)
    grad_mixed = grad_y * gain * scale - mixed * coef

    rate = column(rate_ref[...])
    soft, gate = gates(decay_ref[...], rate)
    slope = jax.nn.sigmoid(decay_ref[...])
    cumul_col, cumul_row = cumul_forms(gate)
    write_all = jax.nn.sigmoid(beta_ref[...])
    row_i = iota((length, length), 0)
    col_i = iota((length, length), 1)
    upper = (row_i <= col_i).astype(F32).astype(BF16)
    gathered = jnp.zeros((length, size), F32)
    half = size // 2

    @pl.when(step == 0)
    def _():
        d_decay_ref[...] = jnp.zeros_like(d_decay_ref)
        d_beta_ref[...] = jnp.zeros_like(d_beta_ref)

    heads = range(group)
    pre = []
    for j in heads:
        cols = slice(j * size, (j + 1) * size)
        head = step * group + j
        col = pick_col(cumul_col, head)
        row = pick_row(cumul_row, head)
        write = column(pick_row(write_all, head))
        spread = jnp.exp(jnp.minimum(col - row, 0.0))
        growth = jnp.exp(col)
        last = col[length - 1 : length, :]
        tail = jnp.exp(last - col)
        query, key = query_ref[j], key_ref[j]
        entering = keep * state_ref[j]
        leaving = grad_ref[j]
        enter_pair, leave_pair = pair(entering), pair(leaving)
        key_pair, query_pair = pair(key), pair(query)
        grad = grad_mixed[:, cols]
        grad_pair = pair(grad)
        delta = base_ref[j] - dot3(pair(reach_key_ref[j]), enter_pair, NT)
        used = write * delta
        used_pair = pair(used)
        d_used = dot3(pair(attn_ref[j]), grad_pair, TN) + tail * dot3(key_pair, leave_pair, NT)
        d_attn = jnp.where(row_i >= col_i, spread * dot3(grad_pair, used_pair, NT), 0.0)
        d_attn_pair = pair(d_attn)
        d_query = growth * dot3(grad_pair, enter_pair, NN) + dot3(d_attn_pair, key_pair, NN)
        d_key_tail = tail * dot3(used_pair, leave_pair, NN)
        d_key_plus = dot3(d_attn_pair, query_pair, TN) + d_key_tail
        right = dot3(pair(inv_ref[j]), pair(write * d_used), TN)
        right_pair = pair(right)
        d_system = jnp.where(row_i > col_i, -spread * dot3(right_pair, pair(delta), NT), 0.0)
        d_system_pair = pair(d_system)
        d_inner = dot3(d_system_pair, key_pair, TN)
        d_key_minus = dot3(d_system_pair, pair(write * key), NN) - growth * dot3(
            right_pair, enter_pair, NN
        )
        d_key_plus = d_key_plus + write * d_inner
        d_write = rows_sum(d_used * delta + key * d_inner)
        whole = jnp.sum(rows_sum(key * d_key_tail), axis=0, keepdims=True) + jnp.exp(
            last
        ) * jnp.sum(rows_sum(leaving * entering), axis=0, keepdims=True)
        d_cumul = rows_sum(query * d_query + key * (d_key_minus - d_key_plus))
        spot = jnp.where(iota(d_cumul.shape, 0) == length - 1, whole, 0.0)
        d_key = d_key_plus + d_key_minus
        gathered = gathered + jnp.where(col_i == head, d_cumul + spot, 0.0)
        gathered = gathered + jnp.where(col_i == half + head, d_write, 0.0)
        pre.append((d_query, d_key, right))

    turned = gathered.T
    count = decay_ref.shape[0]
    d_gate = sum(dot_dims(p, upper, NT) for p in pair(turned[0:count]))
    d_decay_ref[...] += -rate * slope * d_gate
    d_beta_ref[...] += turned[half : half + count] * write_all * (1.0 - write_all)
    d_rate = -rows_sum(soft * d_gate)
    for j in heads:
        one = pick_row(d_rate, step * group + j)
        param_ref[13:14, j * size : (j + 1) * size] = jnp.broadcast_to(one, (1, size))

    rooted = size ** (-0.5)
    back_ref[...] = jnp.zeros_like(back_ref)
    for number, (ref, dst) in enumerate(((q_ref, dq_ref), (k_ref, dk_ref), (v_ref, dv_ref))):
        d_conv[0:8, :] = jnp.zeros((8, width), F32)
        d_conv[8 + length :, :] = jnp.zeros((8, width), F32)
        padded[0:8, :] = halo_ref[number].astype(F32)[TILE - 8 :] * keep
        padded[8 : 8 + length, :] = ref[...].astype(F32)
        for j in heads:
            cols = slice(j * size, (j + 1) * size)
            total = y_ref[number, :, cols]
            gated = jax.nn.sigmoid(total)
            grad = pre[j][number]
            if number < 2:
                act = total * gated
                inv_norm = lax.rsqrt(rows_sum(act * act) + EPS)
                unit = act * inv_norm
                if number == 0:
                    grad = grad * rooted
                grad = inv_norm * (grad - unit * rows_sum(unit * grad))
            d_conv[8 : 8 + length, cols] = grad * (gated * (1.0 + total * (1.0 - gated)))
        grad = d_conv[8 : 8 + length, :]
        extended = conv_ref[number, 0:1, :] * d_conv[0 : 8 + length, :]
        param_ref[4 * number : 4 * number + 1, :] = jnp.sum(
            grad * padded[8 : 8 + length, :], axis=0, keepdims=True
        )
        for tap in range(1, taps):
            extended = extended + conv_ref[number, tap : tap + 1, :] * d_conv[tap : tap + 8 + length, :]
            param_ref[4 * number + tap : 4 * number + tap + 1, :] = jnp.sum(
                grad * padded[8 - tap : 8 - tap + length, :], axis=0, keepdims=True
            )
        dst[...] = extended[8:].astype(BF16)
        edge_ref[8 * number : 8 * number + 8, :] = extended[length:]
        back_ref[8 * number : 8 * number + 8, :] = (keep * extended[0:8]).astype(BF16)


def mixer_kernel(
    count,
    partners,
    pairs,
    group,
    q_ref,
    k_ref,
    v_ref,
    conv_ref,
    decay_ref,
    beta_ref,
    rate_ref,
    reset_ref,
    d_out_ref,
    gain_ref,
    out_ref,
    dq_ref,
    dk_ref,
    dv_ref,
    edge_ref,
    d_decay_ref,
    d_beta_ref,
    total_ref,
    arrived_ref,
    y_ref,
    query_ref,
    key_ref,
    inv_ref,
    attn_ref,
    reach_key_ref,
    base_ref,
    reach_ref,
    mix_ref,
    carry_p_ref,
    carry_q_ref,
    state_ref,
    grad_ref,
    state_land,
    state_out,
    grad_land,
    grad_out,
    mixed_ref,
    stat_ref,
    stat_land,
    halo_ref,
    halo_land,
    back_ref,
    back_land,
    param_ref,
    near_land,
    far_land,
    final_land,
    padded,
    d_conv,
    halo_send,
    halo_recv,
    state_send,
    state_recv,
    grad_send,
    grad_recv,
    stat_send,
    stat_recv,
    near_send,
    near_recv,
    far_send,
    far_recv,
    final_send,
    final_recv,
    back_send,
    back_recv,
):
    place = lax.axis_index("ctx")
    core = lax.axis_index("dp")
    heads, length, size = mix_ref.shape
    steps = heads // group
    span = group * size
    rows = param_ref.shape[0] // pairs
    full_width = heads * size * partners
    raws = (q_ref, k_ref, v_ref)
    kept = (query_ref, key_ref, inv_ref, attn_ref, reach_key_ref, base_ref)
    greet(others("ctx", count) + others("head", partners) + others("dp", pairs))

    def halo_copy(number):
        return pltpu.make_async_remote_copy(
            src_ref=raws[number].at[pl.ds(length - TILE, TILE)],
            dst_ref=halo_land.at[number],
            send_sem=halo_send.at[number],
            recv_sem=halo_recv.at[number],
            device_id={"ctx": lax.rem(place + 1, count)},
            device_id_type=MESH,
        )

    @pl.when(place < count - 1)
    def _():
        for number in range(3):
            halo_copy(number).start()

    @pl.when(place == 0)
    def _():
        halo_ref[...] = jnp.zeros_like(halo_ref)

    @pl.when(place > 0)
    def _():
        for number in range(3):
            halo_copy(number).wait_recv()
        halo_ref[...] = halo_land[...]

    def state_copy(h):
        return pltpu.make_async_remote_copy(
            src_ref=state_out.at[h],
            dst_ref=state_land.at[h],
            send_sem=state_send.at[h],
            recv_sem=state_recv.at[h],
            device_id={"ctx": lax.rem(place + 1, count)},
            device_id_type=MESH,
        )

    def grad_copy(h):
        return pltpu.make_async_remote_copy(
            src_ref=grad_out.at[h],
            dst_ref=grad_land.at[h],
            send_sem=grad_send.at[h],
            recv_sem=grad_recv.at[h],
            device_id={"ctx": lax.rem(place + count - 1, count)},
            device_id_type=MESH,
        )

    def forward(step, carry):
        wide = pl.ds(pl.multiple_of(step * span, span), span)
        some = pl.ds(step * group, group)
        local_part(
            step,
            group,
            *[ref.at[:, wide] for ref in raws],
            halo_ref.at[:, :, wide],
            conv_ref.at[:, :, wide],
            decay_ref,
            beta_ref,
            rate_ref,
            reset_ref,
            y_ref.at[:, :, wide],
            *[ref.at[some] for ref in (*kept, reach_ref, mix_ref, carry_p_ref, carry_q_ref)],
            padded,
        )

        @pl.when(place == 0)
        def _():
            for j in range(group):
                h = step * group + j
                state_ref[h] = jnp.zeros((size, size), F32)
                state_out[h] = carry_q_ref[h]
                if count > 1:
                    state_copy(h).start()

        return carry

    lax.fori_loop(0, steps, forward, 0)

    def enter(h):
        state_copy(h).wait_recv()
        entering = state_land[h]
        state_ref[h] = entering

        @pl.when(place < count - 1)
        def _():
            state_out[h] = carry_q_ref[h] + dot3(pair(entering), pair(carry_p_ref[h]), NN)
            state_copy(h).start()

    def mixing(h, carry):
        square, inner = carry

        @pl.when(place > 0)
        def _():
            enter(h)

        cols = pl.ds(pl.multiple_of(h * size, size), size)
        mixed = mix_ref[h] + dot3(pair(reach_ref[h]), pair(state_ref[h]), NT)
        mixed_ref[:, cols] = mixed
        weighted = d_out_ref[:, cols].astype(F32) * gain_ref[:, cols]
        return square + mixed * mixed, inner + weighted * mixed

    zero = jnp.zeros((length, size), F32)
    square, inner = lax.fori_loop(0, heads, mixing, (zero, zero))
    half = iota((length, size), 1) < size // 2
    mine = lax.axis_index("head")
    stat_land[mine] = jnp.where(half, rows_sum(square), rows_sum(inner))

    def stat_copy(target, slot):
        return pltpu.make_async_remote_copy(
            src_ref=stat_land.at[mine],
            dst_ref=stat_land.at[slot],
            send_sem=stat_send.at[target],
            recv_sem=stat_recv.at[slot],
            device_id={"head": target},
            device_id_type=MESH,
        )

    for step in range(1, partners):
        stat_copy(lax.rem(mine + step, partners), mine).start()
    for step in range(1, partners):
        source = lax.rem(mine + step, partners)
        stat_copy(source, source).wait_recv()
    stat = stat_land[0]
    for slot in range(1, partners):
        stat = stat + stat_land[slot]
    stat_ref[...] = stat
    scale = lax.rsqrt(stat[:, 0:1] / full_width + EPS)
    coef = scale * scale * scale * stat[:, size - 1 : size] / full_width

    def source_grad(h, carry):
        cols = pl.ds(pl.multiple_of(h * size, size), size)
        weighted = d_out_ref[:, cols].astype(F32) * gain_ref[:, cols]
        grad_mixed = weighted * scale - mixed_ref[:, cols] * coef
        grad_out[h] = dot3(pair(grad_mixed), pair(reach_ref[h]), TN)

        @pl.when((place == count - 1) & (place > 0))
        def _():
            grad_copy(h).start()

        return carry

    @pl.when(place > 0)
    def _():
        lax.fori_loop(0, heads, source_grad, 0)

    @pl.when(place == count - 1)
    def _():
        grad_ref[...] = jnp.zeros_like(grad_ref)

    def hop(h, carry):
        grad_copy(h).wait_recv()
        leaving = grad_land[h]
        grad_ref[h] = leaving

        @pl.when(place > 0)
        def _():
            grad_out[h] = grad_out[h] + dot3(pair(leaving), pair(carry_p_ref[h]), NT)
            grad_copy(h).start()

        return carry

    def backward(step, carry):
        wide = pl.ds(pl.multiple_of(step * span, span), span)
        some = pl.ds(step * group, group)

        @pl.when((place < count - 1) & (place > 0) & (step == 0))
        def _():
            lax.fori_loop(0, heads, hop, 0)

        @pl.when((place < count - 1) & (place == 0))
        def _():
            lax.fori_loop(step * group, step * group + group, hop, 0)

        back_part(
            step,
            group,
            full_width,
            *[ref.at[:, wide] for ref in raws],
            halo_ref.at[:, :, wide],
            conv_ref.at[:, :, wide],
            decay_ref,
            beta_ref,
            rate_ref,
            reset_ref,
            d_out_ref.at[:, wide],
            gain_ref.at[:, wide],
            mixed_ref.at[:, wide],
            stat_ref,
            y_ref.at[:, :, wide],
            *[ref.at[some] for ref in (*kept, state_ref, grad_ref)],
            *[ref.at[:, wide] for ref in (out_ref, dq_ref, dk_ref, dv_ref, edge_ref, back_ref, param_ref)],
            d_decay_ref,
            d_beta_ref,
            padded,
            d_conv,
        )
        return carry

    lax.fori_loop(0, steps, backward, 0)

    for step in range(1, partners):
        stat_copy(lax.rem(mine + step, partners), mine).wait_send()

    @pl.when(place < count - 1)
    def _():
        def done(h, carry):
            state_copy(h).wait_send()
            return carry

        lax.fori_loop(0, heads, done, 0)

    @pl.when(place > 0)
    def _():
        def done(h, carry):
            grad_copy(h).wait_send()
            return carry

        lax.fori_loop(0, heads, done, 0)

    back = pltpu.make_async_remote_copy(
        src_ref=back_ref,
        dst_ref=back_land,
        send_sem=back_send,
        recv_sem=back_recv,
        device_id={"ctx": lax.rem(place + count - 1, count)},
        device_id_type=MESH,
    )

    @pl.when(place > 0)
    def _():
        back.start()

    def near(target, slot):
        return pltpu.make_async_remote_copy(
            src_ref=param_ref.at[pl.ds(pl.multiple_of(target * rows, rows), rows)],
            dst_ref=near_land.at[slot],
            send_sem=near_send.at[target],
            recv_sem=near_recv.at[slot],
            device_id={"dp": target},
            device_id_type=MESH,
        )

    def far(target, slot):
        return pltpu.make_async_remote_copy(
            src_ref=far_land.at[place],
            dst_ref=far_land.at[slot],
            send_sem=far_send.at[target],
            recv_sem=far_recv.at[slot],
            device_id={"ctx": target},
            device_id_type=MESH,
        )

    def final(target, slot):
        return pltpu.make_async_remote_copy(
            src_ref=final_land.at[core],
            dst_ref=final_land.at[slot],
            send_sem=final_send.at[target],
            recv_sem=final_recv.at[slot],
            device_id={"dp": target},
            device_id_type=MESH,
        )

    def exchange(copy, here, total):
        for step in range(1, total):
            copy(lax.rem(here + step, total), here).start()
        for step in range(1, total):
            source = lax.rem(here + step, total)
            copy(source, source).wait_recv()

    def settle(copy, here, total):
        for step in range(1, total):
            copy(lax.rem(here + step, total), here).wait_send()

    near_land[core] = param_ref[pl.ds(pl.multiple_of(core * rows, rows), rows), :]
    exchange(near, core, pairs)
    part = near_land[0]
    for slot in range(1, pairs):
        part = part + near_land[slot]
    far_land[place] = part
    exchange(far, place, count)
    part = far_land[0]
    for slot in range(1, count):
        part = part + far_land[slot]
    final_land[core] = part
    exchange(final, core, pairs)
    total_ref[...] = final_land[...]

    @pl.when(place == count - 1)
    def _():
        arrived_ref[...] = jnp.zeros_like(arrived_ref)

    @pl.when(place < count - 1)
    def _():
        back.wait_recv()
        arrived_ref[...] = back_land[...]

    @pl.when(place < count - 1)
    def _():
        for number in range(3):
            halo_copy(number).wait_send()

    settle(near, core, pairs)
    settle(far, place, count)
    settle(final, core, pairs)

    @pl.when(place > 0)
    def _():
        back.wait_send()


def final_kernel(
    o_ref, decay_ref, beta_ref, q_ref, k_ref, v_ref, edge_ref, come_ref, total_ref,
    out_ref, d_decay_ref, d_beta_ref, dq_ref, dk_ref, dv_ref, conv_ref, gain_ref, rate_ref,
):
    out_ref[...] = o_ref[...]
    d_decay_ref[...] = decay_ref[...]
    d_beta_ref[...] = beta_ref[...]
    length, width = q_ref.shape
    numbers, taps = conv_ref.shape[:2]
    heads = rate_ref.shape[1]
    size = width // heads
    for number, (ref, dst) in enumerate(((q_ref, dq_ref), (k_ref, dk_ref), (v_ref, dv_ref))):
        dst[...] = ref[...]
        part = slice(8 * number, 8 * number + 8)
        rows = edge_ref[part, :] + jnp.where(
            iota((8, width), 0) >= 9 - taps, come_ref[...].astype(F32)[part], 0.0
        )
        tile = jnp.concatenate([ref[length - TILE :, :].astype(F32)[0 : TILE - 8], rows], 0)
        dst[length - TILE :, :] = tile.astype(BF16)
    total = total_ref[...]
    for number in range(numbers):
        conv_ref[number] = total[number * taps : (number + 1) * taps]
    gain_ref[...] = total[12:13]
    rate = jnp.zeros(rate_ref.shape, F32)
    for head in range(heads):
        one = total[13:14, head * size : head * size + 1]
        rate = rate + jnp.where(iota(rate.shape, 1) == head, one, 0.0)
    rate_ref[...] = rate


def remote_params(number):
    return pltpu.CompilerParams(
        collective_id=number, has_side_effects=True, vmem_limit_bytes=VMEM_BYTES
    )


def body(
    q_raw,
    k_raw,
    v_raw,
    conv_weight,
    decay_logit,
    beta_logit,
    decay_rate,
    block_resets,
    norm_gain,
    d_out,
):
    tokens, width = q_raw.shape[1:]
    heads = decay_logit.shape[2]
    size = width // heads
    taps = conv_weight.shape[1]
    count = lax.axis_size("ctx")
    partners = lax.axis_size("head")
    pairs = lax.axis_size("dp")
    group = 4 if heads % 4 == 0 else 1
    span = group * size
    vmem = pl.BlockSpec(memory_space=pltpu.VMEM)
    shape = jax.ShapeDtypeStruct
    dma = pltpu.SemaphoreType.DMA
    raws = (q_raw[0], k_raw[0], v_raw[0])
    gain = norm_gain[None, :]
    rate = decay_rate[None, :]
    decay, beta = decay_logit[0].T, beta_logit[0].T

    flag = pl.BlockSpec(memory_space=pltpu.SMEM)
    wide = shape((tokens, width), BF16)
    gate = shape((heads, tokens), F32)
    lines = 16
    part = lines // pairs
    buffer = pltpu.VMEM((heads, tokens, size), F32)
    square = pltpu.VMEM((heads, size, size), F32)
    out, d_q, d_k, d_v, edge, d_decay, d_beta, total, arrived = pl.pallas_call(
        functools.partial(mixer_kernel, count, partners, pairs, group),
        out_shape=[wide] * 4
        + [
            shape((24, width), F32),
            gate,
            gate,
            shape((pairs, part, width), F32),
            shape((32, width), BF16),
        ],
        in_specs=[vmem] * 7 + [flag] + [vmem] * 2,
        out_specs=[vmem] * 9,
        scratch_shapes=[pltpu.VMEM((3, tokens, width), F32)]
        + [buffer] * 8
        + [square] * 8
        + [
            pltpu.VMEM((tokens, width), F32),
            pltpu.VMEM((tokens, size), F32),
            pltpu.VMEM((partners, tokens, size), F32),
            pltpu.VMEM((3, TILE, width), BF16),
            pltpu.VMEM((3, TILE, width), BF16),
            pltpu.VMEM((32, width), BF16),
            pltpu.VMEM((32, width), BF16),
            pltpu.VMEM((lines, width), F32),
            pltpu.VMEM((pairs, part, width), F32),
            pltpu.VMEM((count, part, width), F32),
            pltpu.VMEM((pairs, part, width), F32),
            pltpu.VMEM((tokens + 8, span), F32),
            pltpu.VMEM((tokens + 16, span), F32),
        ]
        + [dma((3,))] * 2
        + [dma((heads,))] * 4
        + [dma((partners,))] * 2
        + [dma((pairs,))] * 2
        + [dma((count,))] * 2
        + [dma((pairs,))] * 2
        + [dma] * 2,
        compiler_params=remote_params(0),
        name="mixer",
    )(*raws, conv_weight, decay, beta, rate, block_resets, d_out[0], gain)
    total = total.reshape(16, width)
    out, d_decay, d_beta, d_q, d_k, d_v, d_conv, d_gain, d_rate = pl.pallas_call(
        final_kernel,
        out_shape=[wide, gate, gate]
        + [wide] * 3
        + [shape((3, taps, width), F32), shape((1, width), F32), shape((1, heads), F32)],
        in_specs=[vmem] * 9,
        out_specs=[vmem] * 9,
        compiler_params=pltpu.CompilerParams(vmem_limit_bytes=VMEM_BYTES),
        name="final",
    )(out, d_decay, d_beta, d_q, d_k, d_v, edge, arrived, total)
    return (
        out[None],
        d_q[None],
        d_k[None],
        d_v[None],
        d_conv,
        d_decay.T[None],
        d_beta.T[None],
        d_rate[0],
        d_gain[0],
    )


def solution(mesh):
    placed = (
        P("dp", "ctx", "head"),
        P("dp", "ctx", "head"),
        P("dp", "ctx", "head"),
        P(None, None, "head"),
        P("dp", "ctx", "head"),
        P("dp", "ctx", "head"),
        P("head"),
        P("dp", "ctx"),
        P("head"),
        P("dp", "ctx", "head"),
    )
    return jax.shard_map(
        body,
        mesh=mesh,
        in_specs=placed,
        out_specs=(
            P("dp", "ctx", "head"),
            P("dp", "ctx", "head"),
            P("dp", "ctx", "head"),
            P("dp", "ctx", "head"),
            P(None, None, "head"),
            P("dp", "ctx", "head"),
            P("dp", "ctx", "head"),
            P("head"),
            P("head"),
        ),
        check_vma=False,
    )
```
